32 devices in a mesh: dp: 8 (over z, x), fsdp: 4 (over y, core).
Axes of the slice: x: 2, y: 2, z: 4, core: 2. Of those that a mesh axis runs over, the one named last changes fastest.
Arguments:
- latents: bfloat16 [16, 512, 1408], P('dp', 'fsdp'), may hold values from -6 to 6
- skip_input: bfloat16 [16, 512, 1408], P('dp', 'fsdp'), may hold values from -6 to 6
- text_tokens: bfloat16 [16, 336, 1024], P('dp', 'fsdp'), may hold values from -6 to 6
- cotangent: bfloat16 [16, 512, 1408], P('dp', 'fsdp'), may hold values from -6 to 6
- timesteps: int32 [16], P('dp'), may hold values from 0 to 999
- text_lengths: int32 [16], P('dp'), may hold values from 84 to 336
- positions: int32 [16, 2, 512], P('dp', None, 'fsdp'), may hold values from 0 to 127, as said below
- skip_weight: float32 [2816, 1408], P('dp', 'fsdp'), as said below
- skip_rows: float32 [2816], P('dp'), may hold values from 81 to 4096
- skip_columns: float32 [1408], P('fsdp'), may hold values from 81 to 4096
- square_weight: float32 [2, 1408, 1408], P(None, 'dp', 'fsdp'), as said below
- square_rows: float32 [2, 1408], P(None, 'dp'), may hold values from 81 to 4096
- square_columns: float32 [2, 1408], P(None, 'fsdp'), may hold values from 81 to 4096
- self_weight: float32 [1408, 4224], P('dp', 'fsdp'), as said below
- self_rows: float32 [1408], P('dp'), may hold values from 81 to 4096
- self_columns: float32 [4224], P('fsdp'), may hold values from 81 to 4096
- output_weight: float32 [2, 1408, 1408], P(None, 'dp', 'fsdp'), as said below
- output_rows: float32 [2, 1408], P(None, 'dp'), may hold values from 81 to 4096
- output_columns: float32 [2, 1408], P(None, 'fsdp'), may hold values from 81 to 4096
- text_weight: float32 [1024, 2816], P('dp', 'fsdp'), as said below
- text_rows: float32 [1024], P('dp'), may hold values from 81 to 4096
- text_columns: float32 [2816], P('fsdp'), may hold values from 81 to 4096
- up_weight: float32 [1408, 6144], P('dp', 'fsdp'), as said below
- up_rows: float32 [1408], P('dp'), may hold values from 81 to 4096
- up_columns: float32 [6144], P('fsdp'), may hold values from 81 to 4096
- down_weight: float32 [6144, 1408], P('dp', 'fsdp'), as said below
- down_rows: float32 [6144], P('dp'), may hold values from 81 to 4096
- down_columns: float32 [1408], P('fsdp'), may hold values from 81 to 4096
- norm_gains: float32 [5, 1408], replicated, may hold values from 0.1 to 1.9
- gain_state: float32 [5, 1408], replicated, may hold values from 81 to 4096
Outputs:
- block_output: bfloat16 [16, 512, 1408], P('dp', 'fsdp')
- latents_grad: bfloat16 [16, 512, 1408], P('dp', 'fsdp')
- skip_input_grad: bfloat16 [16, 512, 1408], P('dp', 'fsdp')
- skip_new: float32 [2816, 1408], P('dp', 'fsdp')
- skip_rows_new: float32 [2816], P('dp')
- skip_columns_new: float32 [1408], P('fsdp')
- skip_gradient: float32 [2816, 1408], P('dp', 'fsdp')
- square_new: float32 [2, 1408, 1408], P(None, 'dp', 'fsdp')
- square_rows_new: float32 [2, 1408], P(None, 'dp')
- square_columns_new: float32 [2, 1408], P(None, 'fsdp')
- square_gradient: float32 [2, 1408, 1408], P(None, 'dp', 'fsdp')
- self_new: float32 [1408, 4224], P('dp', 'fsdp')
- self_rows_new: float32 [1408], P('dp')
- self_columns_new: float32 [4224], P('fsdp')
- self_gradient: float32 [1408, 4224], P('dp', 'fsdp')
- output_new: float32 [2, 1408, 1408], P(None, 'dp', 'fsdp')
- output_rows_new: float32 [2, 1408], P(None, 'dp')
- output_columns_new: float32 [2, 1408], P(None, 'fsdp')
- output_gradient: float32 [2, 1408, 1408], P(None, 'dp', 'fsdp')
- text_new: float32 [1024, 2816], P('dp', 'fsdp')
- text_rows_new: float32 [1024], P('dp')
- text_columns_new: float32 [2816], P('fsdp')
- text_gradient: float32 [1024, 2816], P('dp', 'fsdp')
- up_new: float32 [1408, 6144], P('dp', 'fsdp')
- up_rows_new: float32 [1408], P('dp')
- up_columns_new: float32 [6144], P('fsdp')
- up_gradient: float32 [1408, 6144], P('dp', 'fsdp')
- down_new: float32 [6144, 1408], P('dp', 'fsdp')
- down_rows_new: float32 [6144], P('dp')
- down_columns_new: float32 [1408], P('fsdp')
- down_gradient: float32 [6144, 1408], P('dp', 'fsdp')
- gains_new: float32 [5, 1408], replicated
- gain_state_new: float32 [5, 1408], replicated
- gains_gradient: float32 [5, 1408], replicated
The draws below stay inside these ranges and needn't reach their ends.
Inputs may be any that keep to these rules, and one draw needn't show every extreme that they name: Each latent's tokens lie row by row on a grid of 4, 8, 16 or 32 columns: positions[b, 0] is a token's row and positions[b, 1] its column. Latent 0 has 4 columns and latent 1 has 32. `skip_weight`: independent entries of mean zero. `square_weight`: independent entries of mean zero. `self_weight`: independent entries of mean zero. `output_weight`: independent entries of mean zero. `text_weight`: independent entries of mean zero. `up_weight`: independent entries of mean zero. `down_weight`: independent entries of mean zero.
All inputs are finite; a program needn't handle non-finite values.
Results may differ from the reference program's by a relative error of at most 0.02.
Values may be sent and summed in bfloat16 or wider, within the bound.
No kernel may reach another device: no remote copies, remote signals or barrier semaphores. Data moves between devices by JAX's collectives and lax.ppermute only.
A program may use at most 448 MiB of HBM per device.

```python
import math
import jax
import jax.numpy as jnp
from jax import lax

D = 1408
HEADS = 16
HD = 88
FF = 6144
TD = 1024
TEXT = 336
SEQ = 512
LATENTS = 16


def draw_positions(key, part):
    exponents = jax.random.randint(key, (LATENTS, 1), 2, 6)
    exponents = exponents.at[0, 0].set(2).at[1, 0].set(5)
    grid_width = jnp.power(2, exponents).astype(jnp.int32)
    token_order = jnp.arange(SEQ, dtype=jnp.int32)[None, :]
    row_place = token_order // grid_width
    column_place = token_order % grid_width
    return jnp.stack([row_place, column_place], axis=1).astype(jnp.int32)


def rising(key, array_shape, row_dim, fan_in):
    entries = jnp.clip(jax.random.normal(key, array_shape, jnp.float32), -4.0, 4.0)
    end_ratio = 10.0
    row_count = array_shape[row_dim]
    offsets = (jnp.arange(row_count).astype(jnp.float32) + 0.5) / row_count - 0.5
    scaling = jnp.exp(offsets * math.log(end_ratio))
    broadcast_shape = [1] * len(array_shape)
    broadcast_shape[row_dim] = row_count
    return (entries * scaling.reshape(broadcast_shape) * float(fan_in) ** (-0.5)).astype(jnp.float32)


def draw_skip_weight(key, part):
    return rising(jax.random.fold_in(key, 11), (2 * D, D), 0, 2 * D)


def draw_square_weight(key, part):
    return rising(jax.random.fold_in(key, 12), (2, D, D), 1, D)


def draw_self_weight(key, part):
    return rising(jax.random.fold_in(key, 13), (D, 3 * D), 0, D)


def draw_output_weight(key, part):
    return rising(jax.random.fold_in(key, 14), (2, D, D), 1, max(1, D * 16 // SEQ))


def draw_text_weight(key, part):
    return rising(jax.random.fold_in(key, 15), (TD, 2 * D), 0, TD)


def draw_up_weight(key, part):
    return rising(jax.random.fold_in(key, 16), (D, FF), 0, D)


def draw_down_weight(key, part):
    return rising(jax.random.fold_in(key, 17), (FF, D), 0, FF)


def plant(values, stream_key, least, high):
    dims = values.shape
    spot = [jax.random.randint(jax.random.fold_in(stream_key, axis), (), 0, dims[axis]) for axis in range(len(dims))]
    values = values.at[tuple(spot)].set(least)
    longest = dims.index(max(dims))
    spot[longest] = (spot[longest] + 1) % dims[longest]
    return values.at[tuple(spot)].set(high)


def block_scale(own_key, dims, shards, least, high):
    factor_of = 1.0
    for axis_at, parts in shards:
        steps = jax.random.uniform(jax.random.fold_in(jax.random.fold_in(own_key, 6), axis_at), (parts,), jnp.float32, least / len(shards), high / len(shards))
        factor_of = factor_of * jnp.repeat(jnp.exp(steps), dims[axis_at] // parts).reshape((-1,) + (1,) * (len(dims) - 1 - axis_at))
    return factor_of


def centred(key, shape, deviation, most, shards=(), kind=jnp.bfloat16):
    gain = block_scale(key, shape, shards, -0.22, 0.18) if shards else 1.0
    values = jax.random.normal(key, shape, jnp.float32) * deviation * gain
    return jnp.minimum(jnp.maximum(values, -most), most).astype(kind)


def setup_inputs(seed: int = 0) -> dict:
    key_of = jax.random.split(jax.random.key(seed), 31)
    return {
        "latents": centred(key_of[0], (LATENTS, SEQ, D), 1.0, 6.0, ((0, 8), (1, 4))),
        "skip_input": centred(key_of[1], (LATENTS, SEQ, D), 1.0, 6.0, ((0, 8), (1, 4))),
        "text_tokens": centred(key_of[2], (LATENTS, TEXT, TD), 1.0, 6.0, ((0, 8), (1, 4))),
        "cotangent": centred(key_of[3], (LATENTS, SEQ, D), 1.0, 6.0, ((0, 8), (1, 4))),
        "timesteps": plant(jax.random.randint(key_of[4], (LATENTS,), 0, 1000), jax.random.fold_in(key_of[4], 1), 0, 999).astype(jnp.int32),
        "text_lengths": plant(jax.random.randint(key_of[5], (LATENTS,), TEXT // 4, TEXT + 1), jax.random.fold_in(key_of[5], 1), TEXT // 4, TEXT).astype(jnp.int32),
        "positions": draw_positions(jax.random.fold_in(key_of[30], 71), 0),
        "skip_weight": draw_skip_weight(jax.random.fold_in(key_of[30], 71), 0),
        "skip_rows": jnp.clip(jnp.exp(math.log(4096.0) - 3.923317 * jax.random.uniform(key_of[8], (2 * D,), jnp.float32) ** block_scale(key_of[8], (2 * D,), ((0, 8),), -0.2, 0.2)), 81.0, 4096.0),
        "skip_columns": jnp.clip(jnp.exp(math.log(4096.0) - 3.923317 * jax.random.uniform(key_of[9], (D,), jnp.float32) ** block_scale(key_of[9], (D,), ((0, 4),), -0.2, 0.2)), 81.0, 4096.0),
        "square_weight": draw_square_weight(jax.random.fold_in(key_of[30], 71), 0),
        "square_rows": jnp.clip(jnp.exp(math.log(4096.0) - 3.923317 * jax.random.uniform(key_of[11], (2, D), jnp.float32) ** block_scale(key_of[11], (2, D), ((1, 8),), -0.2, 0.2)), 81.0, 4096.0),
        "square_columns": jnp.clip(jnp.exp(math.log(4096.0) - 3.923317 * jax.random.uniform(key_of[12], (2, D), jnp.float32) ** block_scale(key_of[12], (2, D), ((1, 4),), -0.2, 0.2)), 81.0, 4096.0),
        "self_weight": draw_self_weight(jax.random.fold_in(key_of[30], 71), 0),
        "self_rows": jnp.clip(jnp.exp(math.log(4096.0) - 3.923317 * jax.random.uniform(key_of[14], (D,), jnp.float32) ** block_scale(key_of[14], (D,), ((0, 8),), -0.2, 0.2)), 81.0, 4096.0),
        "self_columns": jnp.clip(jnp.exp(math.log(4096.0) - 3.923317 * jax.random.uniform(key_of[15], (3 * D,), jnp.float32) ** block_scale(key_of[15], (3 * D,), ((0, 4),), -0.2, 0.2)), 81.0, 4096.0),
        "output_weight": draw_output_weight(jax.random.fold_in(key_of[30], 71), 0),
        "output_rows": jnp.clip(jnp.exp(math.log(4096.0) - 3.923317 * jax.random.uniform(key_of[17], (2, D), jnp.float32) ** block_scale(key_of[17], (2, D), ((1, 8),), -0.2, 0.2)), 81.0, 4096.0),
        "output_columns": jnp.clip(jnp.exp(math.log(4096.0) - 3.923317 * jax.random.uniform(key_of[18], (2, D), jnp.float32) ** block_scale(key_of[18], (2, D), ((1, 4),), -0.2, 0.2)), 81.0, 4096.0),
        "text_weight": draw_text_weight(jax.random.fold_in(key_of[30], 71), 0),
        "text_rows": jnp.clip(jnp.exp(math.log(4096.0) - 3.923317 * jax.random.uniform(key_of[20], (TD,), jnp.float32) ** block_scale(key_of[20], (TD,), ((0, 8),), -0.2, 0.2)), 81.0, 4096.0),
        "text_columns": jnp.clip(jnp.exp(math.log(4096.0) - 3.923317 * jax.random.uniform(key_of[21], (2 * D,), jnp.float32) ** block_scale(key_of[21], (2 * D,), ((0, 4),), -0.2, 0.2)), 81.0, 4096.0),
        "up_weight": draw_up_weight(jax.random.fold_in(key_of[30], 71), 0),
        "up_rows": jnp.clip(jnp.exp(math.log(4096.0) - 3.923317 * jax.random.uniform(key_of[23], (D,), jnp.float32) ** block_scale(key_of[23], (D,), ((0, 8),), -0.2, 0.2)), 81.0, 4096.0),
        "up_columns": jnp.clip(jnp.exp(math.log(4096.0) - 3.923317 * jax.random.uniform(key_of[24], (FF,), jnp.float32) ** block_scale(key_of[24], (FF,), ((0, 4),), -0.2, 0.2)), 81.0, 4096.0),
        "down_weight": draw_down_weight(jax.random.fold_in(key_of[30], 71), 0),
        "down_rows": jnp.clip(jnp.exp(math.log(4096.0) - 3.923317 * jax.random.uniform(key_of[26], (FF,), jnp.float32) ** block_scale(key_of[26], (FF,), ((0, 8),), -0.2, 0.2)), 81.0, 4096.0),
        "down_columns": jnp.clip(jnp.exp(math.log(4096.0) - 3.923317 * jax.random.uniform(key_of[27], (D,), jnp.float32) ** block_scale(key_of[27], (D,), ((0, 4),), -0.2, 0.2)), 81.0, 4096.0),
        "norm_gains": jnp.clip(1.0 + 0.18 * jax.random.normal(key_of[28], (5, D), jnp.float32), 0.1, 1.9),
        "gain_state": jnp.clip(jnp.exp(jax.random.uniform(key_of[29], (5, D), jnp.float32, math.log(81.0), math.log(4096.0))), 81.0, 4096.0),
    }


EPS_NORM = 1e-06
EPS_SQUARE = 1e-30
EPS_SCALE = 0.001
DECAY = 0.5
CLIP = 1.0
RATE = 0.5
HIGH = lax.Precision.HIGHEST

@jax.custom_vjp
def low(v):
    return lax.optimization_barrier(v.astype(jnp.bfloat16)).astype(jnp.float32)

@jax.custom_vjp
def low_back(v):
    return v

def low_keep(v):
    return (low(v), None)

def low_pass(kept, grad):
    return (grad,)

def back_keep(v):
    return (v, None)

def back_low(kept, grad):
    return (low(grad),)
low.defvjp(low_keep, low_pass)
low_back.defvjp(back_keep, back_low)

def matmul(left, right):
    return jnp.dot(left, right, precision=HIGH, preferred_element_type=jnp.float32)

def norm_rows(values):
    center = values - lax.optimization_barrier(jnp.mean(values, axis=-1, keepdims=True))
    spread = lax.optimization_barrier(jnp.mean(center * center, axis=-1, keepdims=True))
    return center * lax.rsqrt(spread + EPS_NORM)

def rotary(values, places):
    half_width = values.shape[-1] // 2
    quarter = half_width // 2
    frequency = jnp.exp(-math.log(10000.0) * jnp.arange(quarter).astype(jnp.float32) / quarter)
    pieces = []
    for member in range(2):
        block = values[..., member * half_width:(member + 1) * half_width]
        angles = places[member].astype(jnp.float32)[:, None] * frequency[None, :]
        cosine = jnp.cos(angles)[:, None, :]
        sine = jnp.sin(angles)[:, None, :]
        former = block[..., :quarter]
        latter = block[..., quarter:]
        pieces.append(former * cosine - latter * sine)
        pieces.append(latter * cosine + former * sine)
    return jnp.concatenate(pieces, axis=-1)

def time_embed(step_value, model_width):
    half_width = model_width // 2
    frequency = jnp.exp(-math.log(10000.0) * jnp.arange(half_width).astype(jnp.float32) / half_width)
    angles = step_value.astype(jnp.float32) * frequency
    return jnp.concatenate([jnp.cos(angles), jnp.sin(angles)])

def skip_norm(joined, gain_skip):
    return norm_rows(joined) * gain_skip

def modulated(stream, gain_row, shift_row):
    return norm_rows(stream) * gain_row + shift_row

def gained(stream, gain_row):
    return norm_rows(stream) * gain_row

def head_prep(linear, places, head_count):
    row_count = linear.shape[0]
    shaped = linear.reshape(row_count, head_count, -1)
    return rotary(norm_rows(shaped), places).reshape(row_count, -1)

def head_norm(linear, head_count):
    row_count = linear.shape[0]
    return norm_rows(linear.reshape(row_count, head_count, -1)).reshape(row_count, -1)

def attend(queries, key_rows, value_rows, valid_keys):
    query_count = queries.shape[0]
    shaped_query = queries.reshape(query_count, HEADS, HD)
    shaped_keys = key_rows.reshape(key_rows.shape[0], HEADS, HD)
    shaped_values = value_rows.reshape(value_rows.shape[0], HEADS, HD)
    scores = low_back(jnp.einsum('qhd,khd->hqk', shaped_query, shaped_keys, precision=HIGH) * (1.0 / math.sqrt(HD)))
    if valid_keys is not None:
        scores = jnp.where(valid_keys[None, None, :], scores, -1e+30)
    weights_soft = low(jax.nn.softmax(scores, axis=-1))
    mixture = jnp.einsum('hqk,khd->qhd', weights_soft, shaped_values, precision=HIGH)
    return mixture.reshape(query_count, -1)

def latent_forward(weight_set, gain_set, latent, skipped, text_rows, stamp, text_count, places):
    skip_low, square_low, self_low, output_low, text_low, up_low, down_low = [low(matrix) for matrix in weight_set]
    joined = jnp.concatenate([latent, skipped], axis=-1)
    lowered_skip = low(skip_norm(joined, gain_set[0:2].reshape(-1)))
    stream = low_back(matmul(lowered_skip, skip_low))
    embed_low = low(jax.nn.silu(time_embed(stamp, D)))
    shift_row = matmul(embed_low[None, :], square_low[0])
    lowered_self = low(modulated(stream, gain_set[2], shift_row))
    joint = low_back(matmul(lowered_self, self_low))
    queries = low(head_prep(joint[:, :D], places, HEADS))
    key_rows = low(head_prep(joint[:, D:2 * D], places, HEADS))
    value_rows = low(joint[:, 2 * D:])
    attended = low_back(low(attend(queries, key_rows, value_rows, None)))
    self_stream = stream + low_back(matmul(attended, output_low[0]))
    lowered_cross = low(gained(self_stream, gain_set[3]))
    cross_queries = low(head_prep(low_back(matmul(lowered_cross, square_low[1])), places, HEADS))
    text_joint = low_back(matmul(text_rows, text_low))
    text_keys = low(head_norm(text_joint[:, :D], HEADS))
    text_values = low(text_joint[:, D:])
    valid_keys = jnp.arange(TEXT) < text_count
    cross_attended = low_back(low(attend(cross_queries, text_keys, text_values, valid_keys)))
    cross_stream = self_stream + low_back(matmul(cross_attended, output_low[1]))
    lowered_mlp = low(gained(cross_stream, gain_set[4]))
    hidden = low(jax.nn.gelu(low_back(matmul(lowered_mlp, up_low)), approximate=True))
    return cross_stream + low_back(matmul(hidden, down_low))

def factored(master, gradient, rows_old, columns_old):
    squares = gradient * gradient + EPS_SQUARE
    rows_new = DECAY * rows_old + (1.0 - DECAY) * lax.optimization_barrier(jnp.mean(squares, axis=1))
    columns_new = DECAY * columns_old + (1.0 - DECAY) * lax.optimization_barrier(jnp.mean(squares, axis=0))
    estimate = rows_new[:, None] * columns_new[None, :] / jnp.mean(rows_new)
    update = gradient * lax.rsqrt(estimate)
    ratio = jnp.sqrt(jnp.mean(update * update)) / CLIP
    step_scale = jnp.maximum(EPS_SCALE, jnp.sqrt(jnp.mean(master * master)))
    return (master - RATE * step_scale * update / jnp.maximum(1.0, ratio), rows_new, columns_new)

def reference(latents, skip_input, text_tokens, cotangent, timesteps, text_lengths, positions, skip_weight, skip_rows, skip_columns, square_weight, square_rows, square_columns, self_weight, self_rows, self_columns, output_weight, output_rows, output_columns, text_weight, text_rows, text_columns, up_weight, up_rows, up_columns, down_weight, down_rows, down_columns, norm_gains, gain_state):
    weight_set = (skip_weight, square_weight, self_weight, output_weight, text_weight, up_weight, down_weight)

    def one_latent(carry, packed):
        latent, skipped, text_rows_now, upstream, stamp, text_count, places = packed

        def forward(weights_now, gains_now, latent_now, skipped_now):
            return latent_forward(weights_now, gains_now, latent_now, skipped_now, text_rows_now, stamp, text_count, places)
        result, pullback = jax.vjp(forward, weight_set, norm_gains, latent, skipped)
        weight_grads, gain_grads, latent_grad, skip_grad = pullback(upstream)
        weight_total, gain_total = carry
        weight_total = tuple((total_now + grad_now for total_now, grad_now in zip(weight_total, weight_grads)))
        outs_now = (result.astype(jnp.bfloat16), latent_grad.astype(jnp.bfloat16), skip_grad.astype(jnp.bfloat16))
        return ((weight_total, gain_total + gain_grads), outs_now)
    start = (tuple((jnp.zeros_like(matrix) for matrix in weight_set)), jnp.zeros_like(norm_gains))
    packed_all = (latents.astype(jnp.float32), skip_input.astype(jnp.float32), text_tokens.astype(jnp.float32), cotangent.astype(jnp.float32), timesteps, text_lengths, positions)
    (weight_grads, gains_gradient), (block_output, latents_grad, skip_input_grad) = lax.scan(one_latent, start, packed_all)
    stacked = jax.vmap(factored)
    skip_result = factored(skip_weight, weight_grads[0], skip_rows, skip_columns)
    square_result = stacked(square_weight, weight_grads[1], square_rows, square_columns)
    self_result = factored(self_weight, weight_grads[2], self_rows, self_columns)
    output_result = stacked(output_weight, weight_grads[3], output_rows, output_columns)
    text_result = factored(text_weight, weight_grads[4], text_rows, text_columns)
    up_result = factored(up_weight, weight_grads[5], up_rows, up_columns)
    down_result = factored(down_weight, weight_grads[6], down_rows, down_columns)
    gain_state_new = DECAY * gain_state + (1.0 - DECAY) * (gains_gradient * gains_gradient + EPS_SQUARE)
    gain_update = gains_gradient * lax.rsqrt(gain_state_new)
    gain_ratio = jnp.sqrt(jnp.mean(gain_update * gain_update)) / CLIP
    gain_scale = jnp.maximum(EPS_SCALE, jnp.sqrt(jnp.mean(norm_gains * norm_gains)))
    gains_new = norm_gains - RATE * gain_scale * gain_update / jnp.maximum(1.0, gain_ratio)
    return (block_output, latents_grad, skip_input_grad, skip_result[0], skip_result[1], skip_result[2], weight_grads[0], square_result[0], square_result[1], square_result[2], weight_grads[1], self_result[0], self_result[1], self_result[2], weight_grads[2], output_result[0], output_result[1], output_result[2], weight_grads[3], text_result[0], text_result[1], text_result[2], weight_grads[4], up_result[0], up_result[1], up_result[2], weight_grads[5], down_result[0], down_result[1], down_result[2], weight_grads[6], gains_new, gain_state_new, gains_gradient)
```

```python
import functools
import math

import jax
import jax.numpy as jnp
from jax import lax
from jax.experimental import pallas as pl
from jax.experimental.pallas import tpu as pltpu
from jax.sharding import PartitionSpec as P

D = 1408
HEADS = 16

EPS_NORM = 1e-06
EPS_SQUARE = 1e-30
EPS_SCALE = 0.001
DECAY = 0.5
CLIP = 1.0
RATE = 0.5

BF16 = jnp.bfloat16
F32 = jnp.float32


def matmul(left, right):
    return jnp.dot(left, right, preferred_element_type=F32)


def matmul_left(left, right):
    return lax.dot_general(left, right, (((0,), (0,)), ((), ())), preferred_element_type=F32)


def matmul_right(left, right):
    return lax.dot_general(left, right, (((1,), (1,)), ((), ())), preferred_element_type=F32)


def norm_rows(values):
    center = values - jnp.mean(values, axis=-1, keepdims=True)
    spread = jnp.mean(center * center, axis=-1, keepdims=True)
    return center * lax.rsqrt(spread + EPS_NORM)


def rotary(values, places):
    half_width = values.shape[-1] // 2
    quarter = half_width // 2
    frequency = jnp.exp(-math.log(10000.0) * jnp.arange(quarter).astype(F32) / quarter)
    pieces = []
    for member in range(2):
        block = values[..., member * half_width : (member + 1) * half_width]
        angles = places[member].astype(F32)[:, None] * frequency[None, :]
        cosine = jnp.cos(angles)[:, None, :]
        sine = jnp.sin(angles)[:, None, :]
        former = block[..., :quarter]
        latter = block[..., quarter:]
        pieces.append(former * cosine - latter * sine)
        pieces.append(latter * cosine + former * sine)
    return jnp.concatenate(pieces, axis=-1)


def time_embed(steps, model_width):
    half_width = model_width // 2
    frequency = jnp.exp(-math.log(10000.0) * jnp.arange(half_width).astype(F32) / half_width)
    angles = steps.astype(F32)[:, None] * frequency[None, :]
    return jnp.concatenate([jnp.cos(angles), jnp.sin(angles)], axis=-1)


def skip_norm(joined, gain_skip):
    return norm_rows(joined) * gain_skip


def modulated(stream, gain_row, shift_row):
    return norm_rows(stream) * gain_row + shift_row


def gained(stream, gain_row):
    return norm_rows(stream) * gain_row


def head_prep(linear, places):
    row_count = linear.shape[0]
    shaped = linear.reshape(row_count, HEADS, -1)
    return rotary(norm_rows(shaped), places).reshape(row_count, -1)


def head_norm(linear):
    row_count = linear.shape[0]
    return norm_rows(linear.reshape(row_count, HEADS, -1)).reshape(row_count, -1)


def gelu_tanh(values):
    return jax.nn.gelu(values, approximate=True)


def attend_scores(queries, key_rows, valid_keys):
    query_count = queries.shape[0]
    head_size = queries.shape[1] // HEADS
    shaped_query = queries.reshape(query_count, HEADS, head_size)
    shaped_keys = key_rows.reshape(key_rows.shape[0], HEADS, head_size)
    score_scale = 1.0 / math.sqrt(head_size)
    scores = jnp.einsum("qhd,khd->hqk", shaped_query, shaped_keys, preferred_element_type=F32) * score_scale
    if valid_keys is not None:
        scores = jnp.where(valid_keys[None, None, :], scores, -1e30)
    return scores, shaped_query, shaped_keys, score_scale


def attend_forward(queries, key_rows, value_rows, valid_keys):
    query_count = queries.shape[0]
    scores, _, _, _ = attend_scores(queries, key_rows, valid_keys)
    shaped_values = value_rows.reshape(value_rows.shape[0], HEADS, -1)
    row_top = jnp.max(scores, axis=-1, keepdims=True)
    logsum = row_top + jnp.log(jnp.sum(jnp.exp(scores - row_top), axis=-1, keepdims=True))
    weights_soft = jnp.exp(scores - logsum).astype(BF16)
    mixture = jnp.einsum("hqk,khd->qhd", weights_soft, shaped_values, preferred_element_type=F32)
    return mixture.reshape(query_count, -1).astype(BF16), logsum


def attend_backward(queries, key_rows, value_rows, valid_keys, logsum, grad_mixture):
    query_count = queries.shape[0]
    scores, shaped_query, shaped_keys, score_scale = attend_scores(queries, key_rows, valid_keys)
    shaped_values = value_rows.reshape(value_rows.shape[0], HEADS, -1)
    shaped_grad = grad_mixture.reshape(query_count, HEADS, -1)
    weights_full = jnp.exp(scores - logsum)
    weights_soft = weights_full.astype(BF16)
    grad_weights = jnp.einsum("qhd,khd->hqk", shaped_grad, shaped_values, preferred_element_type=F32)
    grad_values = jnp.einsum("hqk,qhd->khd", weights_soft, shaped_grad, preferred_element_type=F32)
    row_delta = jnp.sum(weights_full * grad_weights, axis=-1, keepdims=True)
    grad_scores = (weights_full * (grad_weights - row_delta)).astype(BF16)
    grad_queries = (
        jnp.einsum("hqk,khd->qhd", grad_scores, shaped_keys, preferred_element_type=F32) * score_scale
    )
    grad_keys = (
        jnp.einsum("hqk,qhd->khd", grad_scores, shaped_query, preferred_element_type=F32) * score_scale
    )
    key_count = key_rows.shape[0]
    return (
        grad_queries.reshape(query_count, -1),
        grad_keys.reshape(key_count, -1),
        grad_values.reshape(key_count, -1),
    )


def swap(value, axis, mask):
    size = lax.axis_size(axis)
    return lax.ppermute(value, axis, [(i, i ^ mask) for i in range(size)])


def masks_of(axis):
    size = lax.axis_size(axis)
    return [1 << b for b in range(size.bit_length() - 1)]


def butterfly(value, axis):
    for mask in masks_of(axis):
        value = value + swap(value, axis, mask)
    return value


CORE = ("fsdp", 1)
YAX = ("fsdp", 2)


class Slots:
    def __init__(self, rows):
        self.rows = rows
        self.size = -(-rows // 64) * 16
        self.offset = rows - 2 * self.size
        self.overlap = 4 * self.size - rows

    def start(self, index):
        return (index % 2) * self.offset + (index // 2) * self.size


def to_slot(block, slots):
    pieces = jnp.stack(
        [lax.slice_in_dim(block, slots.start(f), slots.start(f) + slots.size, axis=1) for f in range(4)]
    )
    got = lax.all_to_all(pieces, "fsdp", 0, 0, tiled=False)
    count, breadth = block.shape[0], block.shape[2]
    return jnp.transpose(got, (1, 2, 0, 3)).reshape(count, slots.size, 4 * breadth)


def from_slot(rows, slots):
    count, size, breadth = rows.shape
    pieces = jnp.transpose(rows.reshape(count, size, 4, breadth // 4), (2, 0, 1, 3))
    got = lax.all_to_all(pieces, "fsdp", 0, 0, tiled=False)
    return jnp.concatenate([got[0], got[2], got[1][:, slots.overlap :], got[3]], axis=1)


def staged(pairs, hold_ref, in_sems, out_sems):
    arrivals = [
        pltpu.make_async_copy(source, hold_ref.at[k], in_sems.at[k]) for k, (source, _, _) in enumerate(pairs)
    ]
    for copy in arrivals:
        copy.start()
    departures = []
    for k, (_, rows, target) in enumerate(pairs):
        arrivals[k].wait()
        held = hold_ref.at[k] if rows is None else hold_ref.at[k, :, rows, :]
        copy = pltpu.make_async_copy(held, target, out_sems.at[k])
        copy.start()
        departures.append(copy)
    for copy in departures:
        copy.wait()


def assemble_kernel(stages, slots, index_ref, own_ref, far_ref, out_ref, hold_ref, in_sems, out_sems):
    here_dp = index_ref[0]
    here_f = index_ref[1]
    half = 1 << len(stages)

    def pairs(f):
        made = []
        for side, ref in ((0, own_ref), (1, far_ref)):
            for k in range(half):
                dp_bits, f_bits = 0, side
                for j, (axis, mask) in enumerate(stages):
                    if (k >> j) & 1:
                        if axis == "dp":
                            dp_bits |= mask
                        else:
                            f_bits |= mask
                source_f = f ^ f_bits
                skip = slots.overlap if source_f == 1 else 0
                row = (here_dp ^ dp_bits) * slots.rows + slots.start(source_f) + skip
                row = pl.multiple_of(row, 16)
                size = slots.size - skip
                made.append((ref.at[k], pl.ds(skip, size), out_ref.at[:, pl.ds(row, size), :]))
        return made

    for f in range(4):

        @pl.when(here_f == f)
        def _():
            staged(pairs(f), hold_ref, in_sems, out_sems)


def assemble(index, own, far, stages, slots):
    half, count, size, breadth = own.shape
    total = lax.axis_size("dp") * slots.rows
    bytes_now = 2 * count * total * breadth
    return pl.pallas_call(
        functools.partial(assemble_kernel, stages, slots),
        out_shape=jax.ShapeDtypeStruct((count, total, breadth), own.dtype),
        in_specs=[
            pl.BlockSpec(memory_space=pltpu.SMEM),
            pl.BlockSpec(memory_space=pl.ANY),
            pl.BlockSpec(memory_space=pl.ANY),
        ],
        out_specs=pl.BlockSpec(memory_space=pl.ANY),
        scratch_shapes=[
            pltpu.VMEM((2 * half, count, size, breadth), own.dtype),
            pltpu.SemaphoreType.DMA((2 * half,)),
            pltpu.SemaphoreType.DMA((2 * half,)),
        ],
        compiler_params=pltpu.CompilerParams(vmem_limit_bytes=24 << 20),
        cost_estimate=pl.CostEstimate(flops=0, bytes_accessed=2 * bytes_now, transcendentals=0),
    )(index, own, far)


def place_kernel(stages, index_ref, own_ref, far_ref, out_ref, hold_ref, in_sems, out_sems):
    here_dp = index_ref[0]
    half = own_ref.shape[0]
    made = []
    for side, ref in ((0, own_ref), (1, far_ref)):
        for k in range(half):
            bits = 0
            for j, (_, mask) in enumerate(stages):
                if ((k + side * half) >> j) & 1:
                    bits |= mask
            made.append((ref.at[k], None, out_ref.at[here_dp ^ bits]))
    staged(made, hold_ref, in_sems, out_sems)


def place(index, own, far, stages):
    half, rows, breadth = own.shape
    return pl.pallas_call(
        functools.partial(place_kernel, stages),
        out_shape=jax.ShapeDtypeStruct((2 * half, rows, breadth), own.dtype),
        in_specs=[
            pl.BlockSpec(memory_space=pltpu.SMEM),
            pl.BlockSpec(memory_space=pl.ANY),
            pl.BlockSpec(memory_space=pl.ANY),
        ],
        out_specs=pl.BlockSpec(memory_space=pl.ANY),
        scratch_shapes=[
            pltpu.VMEM((2 * half, rows, breadth), own.dtype),
            pltpu.SemaphoreType.DMA((2 * half,)),
            pltpu.SemaphoreType.DMA((2 * half,)),
        ],
        compiler_params=pltpu.CompilerParams(vmem_limit_bytes=24 << 20),
        cost_estimate=pl.CostEstimate(flops=0, bytes_accessed=8 * half * rows * breadth, transcendentals=0),
    )(index, own, far)


def double(buffer, stages):
    for axis, mask in stages:
        buffer = jnp.concatenate([buffer, swap(buffer, axis, mask)], axis=0)
    return buffer


def gather_full(index, blocks, stages):
    block = blocks.astype(BF16)
    if not fits(block.shape[1]):
        wide = lax.all_gather(block, "fsdp", axis=2, tiled=True)
        return lax.all_gather(wide, "dp", axis=1, tiled=True)
    slots = Slots(block.shape[1])
    own = double(to_slot(block, slots)[None], stages)
    far = swap(own, *CORE)
    return assemble(index, own, far, stages, slots)


def fits(rows):
    return rows % 16 == 0 and rows >= 64


def gather_dp(index, block, stages):
    if not fits(block.shape[0]):
        return lax.all_gather(block, "dp", axis=0, tiled=False)
    own = double(block[None], stages[:-1])
    far = swap(own, *stages[-1])
    return place(index, own, far, stages)


def total_of(parts):
    value = parts[0].astype(F32)
    for part in parts[1:]:
        value = value + part.astype(F32)
    return value


def halve(parts, axis, mask, choose):
    bit = (lax.axis_index(axis) // mask) % 2
    send = total_of([choose(part, 1 - bit) for part in parts]).astype(BF16)
    received = swap(send, axis, mask)
    return [choose(part, bit) for part in parts] + [received]


def dp_dims(size):
    return (2,) * (size.bit_length() - 1)


def reduce_dp_step(parts, dims_left, mask):
    place_now = dims_left.index(mask)

    def choose(part, bit):
        return lax.dynamic_index_in_dim(part, bit, axis=place_now, keepdims=False)

    left = [other for other in dims_left if other != mask]
    return halve(parts, "dp", mask, choose), left


def reduce_full(gradient, stages):
    count, height, breadth = gradient.shape
    dp = lax.axis_size("dp")
    rows = height // dp
    if not fits(rows):
        low = gradient.astype(BF16)
        thin = lax.psum_scatter(low, "fsdp", scatter_dimension=2, tiled=True)
        return lax.psum_scatter(thin.astype(F32), "dp", scatter_dimension=1, tiled=True)
    slots = Slots(rows)
    dims_left = masks_of("dp")[::-1]
    shaped = gradient.reshape((count,) + dp_dims(dp) + (rows, breadth))
    shaped = jnp.moveaxis(shaped, 0, -3)
    parts = [shaped]

    for axis, mask in stages:
        if axis == "dp":
            parts, dims_left = reduce_dp_step(parts, dims_left, mask)
        else:
            step, size = (slots.offset, 2 * slots.size) if mask == 1 else (slots.size, slots.size)

            def choose(part, bit):
                return lax.dynamic_slice_in_dim(part, bit * step, size, axis=part.ndim - 2)

            parts = halve(parts, axis, mask, choose)
    return from_slot(total_of(parts).astype(BF16), slots).astype(F32)


def reduce_dp(gradient, stages):
    dp, rows, breadth = gradient.shape
    if not fits(rows):
        return lax.psum_scatter(gradient.astype(F32), "dp", scatter_dimension=0, tiled=False)
    dims_left = masks_of("dp")[::-1]
    parts = [gradient.reshape(dp_dims(dp) + (rows, breadth))]
    for _, mask in stages:
        parts, dims_left = reduce_dp_step(parts, dims_left, mask)
    return total_of(parts)


def spread_tokens(rows):
    pair = jnp.concatenate([rows, swap(rows, *YAX)], axis=0)
    return jnp.concatenate([pair, swap(pair, *CORE)], axis=0)


def collect_tokens(partial):
    half = partial.shape[0] // 2
    pair = partial[:half] + swap(partial[half:].astype(BF16), *CORE).astype(F32)
    quarter = half // 2
    return pair[:quarter] + swap(pair[quarter:].astype(BF16), *YAX).astype(F32)


def pick(pair, bit):
    return lax.dynamic_index_in_dim(pair, bit, axis=0, keepdims=False)


def to_latent(pair, y):
    return jnp.concatenate([pick(pair, y), swap(pick(pair, 1 - y), *YAX)], axis=0)


def from_latent(rows, y):
    half = rows.shape[0] // 2
    own = rows[:half]
    other = swap(rows[half:], *YAX)
    return jnp.where(y == 0, jnp.stack([own, other]), jnp.stack([other, own]))


def flatten_all(arrays):
    return jnp.concatenate([matrix.reshape(-1) for matrix in arrays])


def split_all(vector, shapes):
    pieces = []
    offset = 0
    for shape_now in shapes:
        count_now = math.prod(shape_now)
        pieces.append(vector[offset : offset + count_now].reshape(shape_now))
        offset = offset + count_now
    return pieces


def shards(
    latents,
    skip_input,
    text_tokens,
    cotangent,
    timesteps,
    text_lengths,
    positions,
    skip_weight,
    skip_rows,
    skip_columns,
    square_weight,
    square_rows,
    square_columns,
    self_weight,
    self_rows,
    self_columns,
    output_weight,
    output_rows,
    output_columns,
    text_weight,
    text_rows,
    text_columns,
    up_weight,
    up_rows,
    up_columns,
    down_weight,
    down_rows,
    down_columns,
    norm_gains,
    gain_state,
):
    dp = lax.axis_size("dp")
    d_at = lax.axis_index("dp")
    f_at = lax.axis_index("fsdp")
    y_at = f_at // 2
    c_at = f_at % 2
    index = jnp.stack([d_at, f_at]).astype(jnp.int32)

    dp_masks = masks_of("dp")
    high = [("dp", mask) for mask in dp_masks if mask > 1]
    low = ("dp", 1)
    order_a = high + [YAX, low]
    order_b = high + [low, YAX]
    order_m = high + [low]
    back_a = [CORE] + order_a[::-1]
    back_b = [CORE] + order_b[::-1]
    back_m = order_m[::-1]

    joined = jnp.concatenate([to_latent(latents, y_at), to_latent(skip_input, y_at)], axis=-1).astype(F32)
    upstream = to_latent(cotangent, y_at)
    text_local = to_latent(text_tokens, y_at)
    places = to_latent(jnp.swapaxes(positions, 1, 2), y_at).T
    text_count = pick(text_lengths, y_at)

    skip_full = gather_full(index, skip_weight[None], order_a)[0]
    self_full = gather_full(index, self_weight[None], order_b)[0]
    text_full = gather_full(index, text_weight[None], order_a)[0]
    cross_full = gather_full(
        index, jnp.stack([output_weight[0], square_weight[1], output_weight[1]]), order_b
    )
    out_self, square_cross, out_cross = cross_full[0], cross_full[1], cross_full[2]
    rows_d = up_weight.shape[0]
    chunk = down_weight.shape[0] // 4
    per_f = up_weight.shape[1] // (4 * chunk)
    up_pieces = jnp.transpose(up_weight.astype(BF16).reshape(rows_d, per_f, 4, chunk), (2, 0, 1, 3))
    up_got = lax.all_to_all(up_pieces, "fsdp", 0, 0, tiled=False)
    up_block = jnp.transpose(up_got, (1, 0, 2, 3)).reshape(rows_d, 4 * per_f * chunk)
    up_full = gather_dp(index, up_block, order_m).reshape(dp * rows_d, -1)
    down_got = lax.all_to_all(
        down_weight.astype(BF16).reshape(4, chunk, -1), "fsdp", 0, 0, tiled=False
    )
    down_block = jnp.transpose(down_got, (1, 0, 2)).reshape(chunk, D)
    down_full = gather_dp(index, down_block, order_m).reshape(dp * chunk, D)

    steps = double(timesteps[None], [("dp", mask) for mask in dp_masks])
    embed_all = jax.nn.silu(time_embed(steps.reshape(-1), D)).astype(BF16)
    rows_q = square_weight.shape[1]
    columns_q = square_weight.shape[2]
    embed_part = lax.dynamic_slice_in_dim(embed_all, d_at * rows_q, rows_q, axis=1)
    shift_parts = matmul(embed_part, square_weight[0].astype(BF16)).reshape(dp, 2, columns_q)
    for mask in dp_masks[::-1]:
        shift_parts = shift_parts[:mask] + swap(shift_parts[mask:], "dp", mask)
    shift_mine = shift_parts[0]
    shift_four = double(shift_mine[None], [CORE, YAX])
    shift_four = jnp.stack([pick(shift_four, f_at ^ f) for f in range(4)])
    shift_row = pick(jnp.swapaxes(shift_four, 0, 1), y_at).reshape(1, D)

    normed_skip, pull_skip = jax.vjp(skip_norm, joined, norm_gains[0:2].reshape(-1))
    lowered_skip = normed_skip.astype(BF16)
    stream = matmul(lowered_skip, skip_full)
    normed_self, pull_self_norm = jax.vjp(modulated, stream, norm_gains[2], shift_row)
    lowered_self = normed_self.astype(BF16)
    joint = matmul(lowered_self, self_full)

    def prepare(linear):
        return head_prep(linear, places)

    query_rows, pull_query = jax.vjp(prepare, joint[:, :D])
    key_local, pull_key = jax.vjp(prepare, joint[:, D : 2 * D])
    queries = query_rows.astype(BF16)
    key_value = jnp.stack([key_local.astype(BF16), joint[:, 2 * D :].astype(BF16)])
    key_value = jnp.concatenate([key_value, swap(key_value, *CORE)], axis=1)
    key_all, value_all = key_value[0], key_value[1]

    text_joint = matmul(text_local, text_full)
    text_key_local, pull_text_key = jax.vjp(head_norm, text_joint[:, :D])
    text_kv = jnp.stack([text_key_local.astype(BF16), text_joint[:, D:].astype(BF16)])
    text_kv = jnp.concatenate([text_kv, swap(text_kv, *CORE)], axis=1)
    text_key_all, text_value_all = text_kv[0], text_kv[1]

    attended, self_logsum = attend_forward(queries, key_all, value_all, None)
    self_stream = stream + matmul(attended, out_self)
    normed_cross, pull_cross_norm = jax.vjp(gained, self_stream, norm_gains[3])
    lowered_cross = normed_cross.astype(BF16)
    cross_linear = matmul(lowered_cross, square_cross)
    cross_query_rows, pull_cross_query = jax.vjp(prepare, cross_linear)
    cross_queries = cross_query_rows.astype(BF16)
    own_text = text_tokens.shape[1]
    text_slots = jnp.concatenate(
        [(f_at ^ mask) * own_text + jnp.arange(own_text) for mask in (0, 2, 1, 3)]
    )
    valid_keys = text_slots < text_count
    cross_attended, cross_logsum = attend_forward(cross_queries, text_key_all, text_value_all, valid_keys)
    cross_stream = self_stream + matmul(cross_attended, out_cross)
    normed_mlp, pull_mlp_norm = jax.vjp(gained, cross_stream, norm_gains[4])
    lowered_mlp = spread_tokens(normed_mlp.astype(BF16))
    hidden_pre = matmul(lowered_mlp, up_full)
    hidden_rows, pull_gelu = jax.vjp(gelu_tanh, hidden_pre)
    hidden_low = hidden_rows.astype(BF16)
    block_rows = (cross_stream + collect_tokens(matmul(hidden_low, down_full))).astype(BF16)
    block_output = from_latent(block_rows, y_at)

    upstream_all = spread_tokens(upstream)
    grad_hidden = matmul_right(upstream_all, down_full)
    grad_pre = pull_gelu(grad_hidden)[0].astype(BF16)
    grad_mlp_in = collect_tokens(matmul_right(grad_pre, up_full))
    term_down = matmul_left(hidden_low, upstream_all).astype(BF16)
    term_up = matmul_left(lowered_mlp, grad_pre).astype(BF16)
    down_rows_sum = reduce_dp(term_down.reshape(dp, chunk, D), back_m)
    up_rows_sum = reduce_dp(term_up.reshape(dp, rows_d, -1), back_m)

    grad_cross_part, grad_gain_mlp = pull_mlp_norm(grad_mlp_in)
    grad_cross_stream = upstream.astype(F32) + grad_cross_part
    cross_low = grad_cross_stream.astype(BF16)
    grad_cross_att = matmul_right(cross_low, out_cross).astype(BF16)
    term_cross_out = matmul_left(cross_attended, cross_low).astype(BF16)
    grad_cross_q, grad_text_key, grad_text_value = attend_backward(
        cross_queries, text_key_all, text_value_all, valid_keys, cross_logsum, grad_cross_att
    )
    grad_text_kv = jnp.stack([grad_text_key, grad_text_value])
    text_half = grad_text_kv.shape[1] // 2
    grad_text_local = grad_text_kv[:, :text_half] + swap(
        grad_text_kv[:, text_half:].astype(BF16), *CORE
    ).astype(F32)
    grad_cross_linear = pull_cross_query(grad_cross_q)[0].astype(BF16)
    grad_cross_in = matmul_right(grad_cross_linear, square_cross)
    term_cross_query = matmul_left(lowered_cross, grad_cross_linear).astype(BF16)
    grad_self_part, grad_gain_cross = pull_cross_norm(grad_cross_in)
    grad_self_stream = grad_cross_stream + grad_self_part
    self_low = grad_self_stream.astype(BF16)
    grad_self_att = matmul_right(self_low, out_self).astype(BF16)
    term_self_out = matmul_left(attended, self_low).astype(BF16)
    cross_sum = reduce_full(jnp.stack([term_self_out, term_cross_query, term_cross_out]), back_b)
    text_grad_joint = jnp.concatenate(
        [pull_text_key(grad_text_local[0])[0], grad_text_local[1]], axis=-1
    ).astype(BF16)
    text_sum = reduce_full(matmul_left(text_local, text_grad_joint).astype(BF16)[None], back_a)

    grad_query, grad_key_all, grad_value_all = attend_backward(
        queries, key_all, value_all, None, self_logsum, grad_self_att
    )
    grad_kv = jnp.stack([grad_key_all, grad_value_all])
    token_half = grad_kv.shape[1] // 2
    grad_kv_local = grad_kv[:, :token_half] + swap(grad_kv[:, token_half:].astype(BF16), *CORE).astype(F32)
    grad_joint = jnp.concatenate(
        [pull_query(grad_query)[0], pull_key(grad_kv_local[0])[0], grad_kv_local[1]], axis=-1
    ).astype(BF16)
    self_sum = reduce_full(matmul_left(lowered_self, grad_joint).astype(BF16)[None], back_b)
    grad_self_in = matmul_right(grad_joint, self_full)
    grad_stream_part, grad_gain_self, grad_shift = pull_self_norm(grad_self_in)
    grad_stream = grad_self_stream + grad_stream_part
    stream_low = grad_stream.astype(BF16)
    skip_sum = reduce_full(matmul_left(lowered_skip, stream_low).astype(BF16)[None], back_a)
    grad_joined, grad_gain_skip = pull_skip(matmul_right(stream_low, skip_full))
    latents_grad = from_latent(grad_joined[:, :D].astype(BF16), y_at)
    skip_input_grad = from_latent(grad_joined[:, D:].astype(BF16), y_at)

    grad_shift = grad_shift.reshape(1, D)
    grad_shift = grad_shift + swap(grad_shift, *CORE)
    other_shift = swap(grad_shift, *YAX)
    shift_pair = jnp.where(
        y_at == 0,
        jnp.concatenate([grad_shift, other_shift]),
        jnp.concatenate([other_shift, grad_shift]),
    )
    shift_pair = lax.dynamic_slice_in_dim(shift_pair, f_at * columns_q, columns_q, axis=1)
    shift_grads = double(shift_pair[None], [("dp", mask) for mask in dp_masks]).reshape(-1, columns_q)
    modulate_sum = lax.dot_general(
        embed_part.astype(F32),
        shift_grads,
        (((0,), (0,)), ((), ())),
        precision=lax.Precision.HIGHEST,
        preferred_element_type=F32,
    )

    up_back = jnp.transpose(
        up_rows_sum.astype(BF16).reshape(rows_d, 4, per_f, chunk), (1, 0, 2, 3)
    )
    up_back = lax.all_to_all(up_back, "fsdp", 0, 0, tiled=False)
    up_sum = jnp.transpose(up_back, (1, 2, 0, 3)).reshape(up_weight.shape).astype(F32)
    down_back = jnp.transpose(down_rows_sum.astype(BF16).reshape(chunk, 4, -1), (1, 0, 2))
    down_back = lax.all_to_all(down_back, "fsdp", 0, 0, tiled=False)
    down_sum = down_back.reshape(down_weight.shape).astype(F32)

    fsdp = lax.axis_size("fsdp")
    master_slabs = [
        skip_weight[None],
        square_weight,
        self_weight[None],
        output_weight,
        text_weight[None],
        up_weight[None],
        down_weight[None],
    ]
    grad_slabs = [
        skip_sum,
        jnp.stack([modulate_sum, cross_sum[1]]),
        self_sum,
        jnp.stack([cross_sum[0], cross_sum[2]]),
        text_sum,
        up_sum[None],
        down_sum[None],
    ]
    row_slabs = [
        skip_rows[None],
        square_rows,
        self_rows[None],
        output_rows,
        text_rows[None],
        up_rows[None],
        down_rows[None],
    ]
    column_slabs = [
        skip_columns[None],
        square_columns,
        self_columns[None],
        output_columns,
        text_columns[None],
        up_columns[None],
        down_columns[None],
    ]
    squares = [gradient * gradient + EPS_SQUARE for gradient in grad_slabs]
    row_parts = [jnp.sum(square_block, axis=2) for square_block in squares]
    column_parts = [jnp.sum(square_block, axis=1) for square_block in squares]
    heights = [part.shape[1] * dp for part in row_parts]
    breadths = [part.shape[1] * fsdp for part in column_parts]
    gains_part = jnp.concatenate(
        [grad_gain_skip.reshape(2, -1), grad_gain_self[None], grad_gain_cross[None], grad_gain_mlp[None]],
        axis=0,
    )
    old_sums = jnp.concatenate([jnp.sum(state, axis=1) for state in row_slabs])
    master_squares = jnp.concatenate([jnp.sum(master * master, axis=(1, 2)) for master in master_slabs])
    early = butterfly(jnp.concatenate([old_sums / fsdp, master_squares]), "fsdp")
    early = butterfly(early, "dp")
    matrix_count = old_sums.shape[0]
    old_total, master_all = early[:matrix_count], early[matrix_count:]

    rows_vector = butterfly(flatten_all(row_parts), "fsdp")
    row_sums = split_all(rows_vector, [part.shape for part in row_parts])
    square_sums = jnp.concatenate([jnp.sum(part, axis=1) for part in row_sums])
    column_shapes = [part.shape for part in column_parts]
    columns_vector = butterfly(
        flatten_all(column_parts + [square_sums, gains_part]), "dp"
    )
    column_all = split_all(columns_vector, column_shapes + [square_sums.shape, gains_part.shape])
    column_sums, square_total, gain_half = column_all[:-2], column_all[-2], column_all[-1]
    gain_total = butterfly(gain_half, "fsdp")

    slab_counts = [(part.shape[0],) for part in row_parts]
    rows_new = [
        DECAY * old_state + (1.0 - DECAY) * summed / breadth
        for old_state, summed, breadth in zip(row_slabs, row_sums, breadths)
    ]
    columns_new = [
        DECAY * old_state + (1.0 - DECAY) * summed / height
        for old_state, summed, height in zip(column_slabs, column_sums, heights)
    ]
    row_means = [
        (DECAY * old_part + (1.0 - DECAY) * square_part / breadth) / height
        for old_part, square_part, breadth, height in zip(
            split_all(old_total, slab_counts), split_all(square_total, slab_counts), breadths, heights
        )
    ]
    updates = [
        gradient * lax.rsqrt(state_row[:, :, None] * state_column[:, None, :] / mean_now[:, None, None])
        for gradient, state_row, state_column, mean_now in zip(grad_slabs, rows_new, columns_new, row_means)
    ]
    update_squares = jnp.concatenate([jnp.sum(update * update, axis=(1, 2)) for update in updates])
    update_all = butterfly(butterfly(update_squares, "fsdp"), "dp")
    new_masters = []
    for master, update, update_sum, master_sum, height, breadth in zip(
        master_slabs,
        updates,
        split_all(update_all, slab_counts),
        split_all(master_all, slab_counts),
        heights,
        breadths,
    ):
        entries = height * breadth
        ratio = jnp.sqrt(update_sum / entries) / CLIP
        step_scale = jnp.maximum(EPS_SCALE, jnp.sqrt(master_sum / entries))
        new_masters.append(
            master - (RATE * step_scale / jnp.maximum(1.0, ratio))[:, None, None] * update
        )
    gain_state_new = DECAY * gain_state + (1.0 - DECAY) * (gain_total * gain_total + EPS_SQUARE)
    gain_update = gain_total * lax.rsqrt(gain_state_new)
    gain_ratio = jnp.sqrt(jnp.mean(gain_update * gain_update)) / CLIP
    gain_scale = jnp.maximum(EPS_SCALE, jnp.sqrt(jnp.mean(norm_gains * norm_gains)))
    gains_new = norm_gains - RATE * gain_scale * gain_update / jnp.maximum(1.0, gain_ratio)
    results = [block_output, latents_grad, skip_input_grad]
    for which in range(7):
        group = [new_masters[which], rows_new[which], columns_new[which], grad_slabs[which]]
        if which in (1, 3):
            results.extend(group)
        else:
            results.extend(item[0] for item in group)
    return tuple(results) + (gains_new, gain_state_new, gain_total)


def solution(mesh):
    matrix, row, column = P("dp", "fsdp"), P("dp"), P("fsdp")
    pair, pair_row, pair_column = P(None, "dp", "fsdp"), P(None, "dp"), P(None, "fsdp")
    tokens = P("dp", "fsdp", None)
    kinds = (False, True, False, True, False, False, False)
    in_specs = [tokens] * 4 + [P("dp"), P("dp"), P("dp", None, "fsdp")]
    out_specs = [tokens] * 3
    for paired in kinds:
        if paired:
            in_specs += [pair, pair_row, pair_column]
            out_specs += [pair, pair_row, pair_column, pair]
        else:
            in_specs += [matrix, row, column]
            out_specs += [matrix, row, column, matrix]
    return jax.shard_map(
        shards,
        mesh=mesh,
        in_specs=tuple(in_specs + [P(), P()]),
        out_specs=tuple(out_specs + [P(), P(), P()]),
        check_vma=False,
    )
```

```python
import functools
import math

import jax
import jax.numpy as jnp
from jax import lax
from jax.experimental import pallas as pl
from jax.experimental.pallas import tpu as pltpu
from jax.sharding import PartitionSpec as P

D = 1408
HEADS = 16

EPS_NORM = 1e-06
EPS_SQUARE = 1e-30
EPS_SCALE = 0.001
DECAY = 0.5
CLIP = 1.0
RATE = 0.5

BF16 = jnp.bfloat16
F32 = jnp.float32


def matmul(left, right):
    return jnp.dot(left, right, preferred_element_type=F32)


def matmul_left(left, right):
    return lax.dot_general(left, right, (((0,), (0,)), ((), ())), preferred_element_type=F32)


def matmul_right(left, right):
    return lax.dot_general(left, right, (((1,), (1,)), ((), ())), preferred_element_type=F32)


def norm_rows(values):
    center = values - jnp.mean(values, axis=-1, keepdims=True)
    spread = jnp.mean(center * center, axis=-1, keepdims=True)
    return center * lax.rsqrt(spread + EPS_NORM)


def rotary(values, places):
    half_width = values.shape[-1] // 2
    quarter = half_width // 2
    frequency = jnp.exp(-math.log(10000.0) * jnp.arange(quarter).astype(F32) / quarter)
    pieces = []
    for member in range(2):
        block = values[..., member * half_width : (member + 1) * half_width]
        angles = places[member].astype(F32)[:, None] * frequency[None, :]
        cosine = jnp.cos(angles)[:, None, :]
        sine = jnp.sin(angles)[:, None, :]
        former = block[..., :quarter]
        latter = block[..., quarter:]
        pieces.append(former * cosine - latter * sine)
        pieces.append(latter * cosine + former * sine)
    return jnp.concatenate(pieces, axis=-1)


def time_embed(steps, model_width):
    half_width = model_width // 2
    frequency = jnp.exp(-math.log(10000.0) * jnp.arange(half_width).astype(F32) / half_width)
    angles = steps.astype(F32)[:, None] * frequency[None, :]
    return jnp.concatenate([jnp.cos(angles), jnp.sin(angles)], axis=-1)


def skip_norm(joined, gain_skip):
    return norm_rows(joined) * gain_skip


def modulated(stream, gain_row, shift_row):
    return norm_rows(stream) * gain_row + shift_row


def gained(stream, gain_row):
    return norm_rows(stream) * gain_row


def head_prep(linear, places):
    row_count = linear.shape[0]
    shaped = linear.reshape(row_count, HEADS, -1)
    return rotary(norm_rows(shaped), places).reshape(row_count, -1)


def head_norm(linear):
    row_count = linear.shape[0]
    return norm_rows(linear.reshape(row_count, HEADS, -1)).reshape(row_count, -1)


def gelu_tanh(values):
    return jax.nn.gelu(values, approximate=True)


def attend_scores(queries, key_rows, valid_keys):
    query_count = queries.shape[0]
    head_size = queries.shape[1] // HEADS
    shaped_query = queries.reshape(query_count, HEADS, head_size)
    shaped_keys = key_rows.reshape(key_rows.shape[0], HEADS, head_size)
    score_scale = 1.0 / math.sqrt(head_size)
    scores = jnp.einsum("qhd,khd->hqk", shaped_query, shaped_keys, preferred_element_type=F32) * score_scale
    if valid_keys is not None:
        scores = jnp.where(valid_keys[None, None, :], scores, -1e30)
    return scores, shaped_query, shaped_keys, score_scale


def attend_forward(queries, key_rows, value_rows, valid_keys):
    query_count = queries.shape[0]
    scores, _, _, _ = attend_scores(queries, key_rows, valid_keys)
    shaped_values = value_rows.reshape(value_rows.shape[0], HEADS, -1)
    row_top = jnp.max(scores, axis=-1, keepdims=True)
    logsum = row_top + jnp.log(jnp.sum(jnp.exp(scores - row_top), axis=-1, keepdims=True))
    weights_soft = jnp.exp(scores - logsum).astype(BF16)
    mixture = jnp.einsum("hqk,khd->qhd", weights_soft, shaped_values, preferred_element_type=F32)
    return mixture.reshape(query_count, -1).astype(BF16), logsum


def attend_backward(queries, key_rows, value_rows, valid_keys, logsum, grad_mixture):
    query_count = queries.shape[0]
    scores, shaped_query, shaped_keys, score_scale = attend_scores(queries, key_rows, valid_keys)
    shaped_values = value_rows.reshape(value_rows.shape[0], HEADS, -1)
    shaped_grad = grad_mixture.reshape(query_count, HEADS, -1)
    weights_full = jnp.exp(scores - logsum)
    weights_soft = weights_full.astype(BF16)
    grad_weights = jnp.einsum("qhd,khd->hqk", shaped_grad, shaped_values, preferred_element_type=F32)
    grad_values = jnp.einsum("hqk,qhd->khd", weights_soft, shaped_grad, preferred_element_type=F32)
    row_delta = jnp.sum(weights_full * grad_weights, axis=-1, keepdims=True)
    grad_scores = (weights_full * (grad_weights - row_delta)).astype(BF16)
    grad_queries = (
        jnp.einsum("hqk,khd->qhd", grad_scores, shaped_keys, preferred_element_type=F32) * score_scale
    )
    grad_keys = (
        jnp.einsum("hqk,qhd->khd", grad_scores, shaped_query, preferred_element_type=F32) * score_scale
    )
    key_count = key_rows.shape[0]
    return (
        grad_queries.reshape(query_count, -1),
        grad_keys.reshape(key_count, -1),
        grad_values.reshape(key_count, -1),
    )


def swap(value, axis, mask):
    size = lax.axis_size(axis)
    return lax.ppermute(value, axis, [(i, i ^ mask) for i in range(size)])


def masks_of(axis):
    size = lax.axis_size(axis)
    return [1 << b for b in range(size.bit_length() - 1)]


def butterfly(value, axis):
    for mask in masks_of(axis):
        value = value + swap(value, axis, mask)
    return value


def after(value, *others):
    others = [other for other in others if other is not None]
    if not others:
        return value
    return lax.optimization_barrier((value, *others))[0]


class Links:
    def __init__(self, depth=2):
        self.depth = depth
        self.sent = {}
        self.gate = None

    def hold(self, value, link):
        queue = self.sent.setdefault(link, [])
        earlier = queue[-self.depth] if len(queue) >= self.depth else None
        return after(value, earlier, self.gate)

    def send(self, value, axis, pairs, link):
        got = lax.ppermute(value, axis, pairs)
        self.sent.setdefault(link, []).append(got)
        return got

    def move(self, value, axis, pairs, link):
        return self.send(self.hold(value, link), axis, pairs, link)

    def swap(self, value, axis, mask):
        return self.move(value, axis, xor_pairs(axis, mask), (axis, mask))


def xor_pairs(axis, mask):
    return [(i, i ^ mask) for i in range(lax.axis_size(axis))]


class Flow:
    def __init__(self, stages):
        self.stages = stages
        self.pending = []
        self.result = None

    def step(self, main=None):
        if self.result is not None:
            return main
        if main is not None:
            main = after(main, *self.pending)
        try:
            self.pending = next(self.stages)
        except StopIteration as end:
            self.pending = []
            self.result = end.value
        return main

    def finish(self):
        while self.result is None:
            self.step()
        return self.result


MIDDLE = [(2, 4), (3, 5), (4, 2), (5, 3)]
OUTWARD = [(2, 0), (3, 1), (4, 6), (5, 7)]
INWARD = [(0, 2), (1, 3), (6, 4), (7, 5)]


CORE = ("fsdp", 1)
YAX = ("fsdp", 2)


class Slots:
    def __init__(self, rows, plain=False, size=None):
        self.rows = rows
        self.plain = plain
        self.size = rows // 4 if plain else size or -(-rows // 64) * 16
        self.offset = rows - 2 * self.size
        self.overlap = 4 * self.size - rows

    def skip(self, index):
        if self.plain or index % 2 == 0:
            return 0
        return min(self.size, max(0, 2 * self.size - self.start(index)))

    def start(self, index):
        if self.plain:
            return index * self.size
        return (index % 2) * self.offset + (index // 2) * self.size


def exchange(pieces, gate=None):
    widest = max(piece.shape[2] for piece in pieces)
    joined = jnp.concatenate(
        [jnp.pad(piece, ((0, 0), (0, 0), (0, widest - piece.shape[2]))) for piece in pieces], axis=1
    )
    got = lax.all_to_all(after(joined, gate), "fsdp", 0, 0, tiled=False)
    made = []
    offset = 0
    for piece in pieces:
        made.append(got[:, offset : offset + piece.shape[1], : piece.shape[2]])
        offset += piece.shape[1]
    return made


def slot_pieces(block, slots):
    count, _, breadth = block.shape
    chunk = D // 4
    cuts = jnp.stack(
        [lax.slice_in_dim(block, slots.start(f), slots.start(f) + slots.size, axis=1) for f in range(4)]
    )
    cuts = cuts.reshape(4, count, slots.size, breadth // chunk, chunk)
    return jnp.swapaxes(cuts, 2, 3).reshape(4, -1, chunk)


def slot_rows(got, slots, count):
    chunk = got.shape[2]
    shaped = got.reshape(4, count, -1, slots.size, chunk)
    return jnp.transpose(shaped, (1, 3, 0, 2, 4)).reshape(count, slots.size, -1)


def back_pieces(rows):
    count, size, breadth = rows.shape
    chunk = D // 4
    shaped = rows.reshape(count, size, 4, breadth // (4 * chunk), chunk)
    return jnp.transpose(shaped, (2, 0, 3, 1, 4)).reshape(4, -1, chunk)


def back_block(got, slots, count):
    chunk = got.shape[2]
    shaped = jnp.swapaxes(got.reshape(4, count, -1, slots.size, chunk), 2, 3)
    shaped = shaped.reshape(4, count, slots.size, -1)
    if slots.plain:
        return jnp.swapaxes(shaped, 0, 1).reshape(count, slots.rows, -1)
    return jnp.concatenate(
        [shaped[0], shaped[2], shaped[1][:, slots.overlap :], shaped[3]], axis=1
    )


def staged(pairs, in_sems, out_sems):
    arrivals = [
        pltpu.make_async_copy(source, hold, in_sems.at[k]) for k, (source, hold, _, _) in enumerate(pairs)
    ]
    for copy in arrivals:
        copy.start()
    departures = []
    for k, (_, _, held, target) in enumerate(pairs):
        arrivals[k].wait()
        copy = pltpu.make_async_copy(held, target, out_sems.at[k])
        copy.start()
        departures.append(copy)
    for copy in departures:
        copy.wait()


def z_sources(z_at):
    return [z_at, z_at ^ 1, jnp.where(z_at < 2, 2, 1), jnp.where(z_at < 2, 3, 0)]


def assemble_kernel(groups, index_ref, *refs):
    here_z = index_ref[0] // 2
    here_x = index_ref[0] % 2
    here_f = index_ref[1]
    out_refs = refs[8 : 8 + len(groups)]
    hold_ref, in_sems, out_sems = refs[8 + len(groups) :]
    sources = z_sources(here_z)

    def copies(f):
        arrivals, departures = [], []
        for side in range(8):
            source_f = f ^ (side // 4) ^ (side & 2)
            for k in range(4):
                source_dp = 2 * sources[k] + (here_x ^ (side & 1))
                at = side * 4 + k
                arrivals.append(pltpu.make_async_copy(refs[side].at[k], hold_ref.at[at], in_sems.at[at]))
                leaving = []
                for which, (first, count, slots) in enumerate(groups):
                    skip = slots.skip(source_f)
                    if skip == slots.size:
                        continue
                    row = source_dp * slots.rows + slots.start(source_f) + skip
                    row = pl.multiple_of(row, 16)
                    size = slots.size - skip
                    leaving.append(
                        pltpu.make_async_copy(
                            hold_ref.at[at, pl.ds(first, count), pl.ds(skip, size), :],
                            out_refs[which].at[:, pl.ds(row, size), :],
                            out_sems.at[at * len(groups) + which],
                        )
                    )
                departures.append(leaving)
        return arrivals, departures

    for f in range(4):

        @pl.when(here_f == f)
        def _():
            arrivals, departures = copies(f)
            for copy in arrivals:
                copy.start()
            for copy, leaving in zip(arrivals, departures):
                copy.wait()
                for onward in leaving:
                    onward.start()
            for leaving in departures:
                for onward in leaving:
                    onward.wait()


def assemble(index, parts, groups):
    _, total, size, breadth = parts[0].shape
    return pl.pallas_call(
        functools.partial(assemble_kernel, groups),
        out_shape=[
            jax.ShapeDtypeStruct((count, 8 * slots.rows, breadth), BF16) for _, count, slots in groups
        ],
        in_specs=[pl.BlockSpec(memory_space=pltpu.SMEM)] + [pl.BlockSpec(memory_space=pl.ANY)] * 8,
        out_specs=[pl.BlockSpec(memory_space=pl.ANY)] * len(groups),
        scratch_shapes=[
            pltpu.VMEM((32, total, size, breadth), BF16),
            pltpu.SemaphoreType.DMA((32,)),
            pltpu.SemaphoreType.DMA((32 * len(groups),)),
        ],
        compiler_params=pltpu.CompilerParams(vmem_limit_bytes=32 << 20),
        cost_estimate=pl.CostEstimate(
            flops=0, bytes_accessed=128 * total * size * breadth, transcendentals=0
        ),
    )(index, *parts)


def assemble_halves_kernel(orders, slots, index_ref, *refs):
    here_z = index_ref[0] // 2
    here_x = index_ref[0] % 2
    here_f = index_ref[1]
    count = len(orders)
    part_refs, out_ref = refs[: 4 * count], refs[4 * count]
    holds, (in_sems, out_sems) = refs[4 * count + 1 : 5 * count + 1], refs[5 * count + 1 :]
    sources = z_sources(here_z)

    def pairs(f):
        made = []
        left = 0
        for which, y_first in enumerate(orders):
            width = part_refs[4 * which].shape[-1]
            for side in range(4):
                ref = part_refs[4 * which + side]
                for k in range(8):
                    bits = (k // 4, side % 2)
                    y_bit, x_bit = bits if y_first else bits[::-1]
                    source_f = f ^ (side // 2) ^ (2 * y_bit)
                    source_dp = 2 * sources[k % 4] + (here_x ^ x_bit)
                    skip = slots.skip(source_f)
                    row = source_dp * slots.rows + slots.start(source_f) + skip
                    row = pl.multiple_of(row, 16)
                    size = slots.size - skip
                    hold = holds[which].at[side * 8 + k]
                    made.append(
                        (
                            ref.at[k],
                            hold,
                            holds[which].at[side * 8 + k, :, pl.ds(skip, size), :],
                            out_ref.at[:, pl.ds(row, size), pl.ds(left, width)],
                        )
                    )
            left += width
        return made

    for f in range(4):

        @pl.when(here_f == f)
        def _():
            staged(pairs(f), in_sems, out_sems)


def assemble_halves(index, parts, orders, slots):
    count, size = parts[0].shape[1:3]
    total = lax.axis_size("dp") * slots.rows
    breadth = sum(part.shape[-1] for part in parts[::4])
    bytes_now = 2 * count * total * breadth
    copies = 32 * len(orders)
    return pl.pallas_call(
        functools.partial(assemble_halves_kernel, orders, slots),
        out_shape=jax.ShapeDtypeStruct((count, total, breadth), BF16),
        in_specs=[pl.BlockSpec(memory_space=pltpu.SMEM)] + [pl.BlockSpec(memory_space=pl.ANY)] * len(parts),
        out_specs=pl.BlockSpec(memory_space=pl.ANY),
        scratch_shapes=[pltpu.VMEM((32, count, size, part.shape[-1]), BF16) for part in parts[::4]]
        + [pltpu.SemaphoreType.DMA((copies,)), pltpu.SemaphoreType.DMA((copies,))],
        compiler_params=pltpu.CompilerParams(vmem_limit_bytes=24 << 20),
        cost_estimate=pl.CostEstimate(flops=0, bytes_accessed=2 * bytes_now, transcendentals=0),
    )(index, *parts)


def place_kernel(index_ref, *refs):
    parts, (out_ref, hold_ref, in_sems, out_sems) = refs[:-4], refs[-4:]
    sources = z_sources(index_ref[0] // 2)
    here_x = index_ref[0] % 2
    made = []
    for side in range(2):
        for k in range(4):
            hold = hold_ref.at[k + side * 4]
            source = parts[side].at[k] if len(parts) == 2 else parts[0].at[k, side]
            made.append((source, hold, hold, out_ref.at[2 * sources[k] + (here_x ^ side)]))
    staged(made, in_sems, out_sems)


def place(index, *parts):
    rows, breadth = parts[0].shape[-2:]
    return pl.pallas_call(
        place_kernel,
        out_shape=jax.ShapeDtypeStruct((8, rows, breadth), BF16),
        in_specs=[pl.BlockSpec(memory_space=pltpu.SMEM)] + [pl.BlockSpec(memory_space=pl.ANY)] * len(parts),
        out_specs=pl.BlockSpec(memory_space=pl.ANY),
        scratch_shapes=[
            pltpu.VMEM((8, rows, breadth), BF16),
            pltpu.SemaphoreType.DMA((8,)),
            pltpu.SemaphoreType.DMA((8,)),
        ],
        compiler_params=pltpu.CompilerParams(vmem_limit_bytes=24 << 20),
        cost_estimate=pl.CostEstimate(flops=0, bytes_accessed=32 * rows * breadth, transcendentals=0),
    )(index, *parts)


def double(buffer, stages):
    for axis, mask in stages:
        buffer = jnp.concatenate([buffer, swap(buffer, axis, mask)], axis=0)
    return buffer


def fits(rows):
    return lax.axis_size("dp") == 8 and rows % 16 == 0 and rows >= 64


def along_z(links, buffer):
    got = links.swap(buffer, "dp", 2)
    yield [got]
    pair = jnp.stack([buffer, got])
    middle = links.move(pair, "dp", MIDDLE, "middle")
    yield [middle]
    outer = links.move(middle, "dp", OUTWARD, ("dp", 2))
    yield [outer]
    z_at = lax.axis_index("dp") // 2
    inner = (z_at == 1) | (z_at == 2)

    def columns(first, last):
        far = jnp.where(inner, middle[..., first:last], outer[..., first:last])
        return jnp.concatenate([pair[..., first:last], far], axis=0)

    return columns


def cut_of(breadth):
    return (breadth // 128 + 1) // 2 * 128


def across(links, value):
    pairs = [(i, i ^ 6) for i in range(4 * lax.axis_size("dp"))]
    got_x, got_y = links.swap(value, "dp", 1), links.swap(value, *YAX)
    return got_x, got_y, links.move(value, ("dp", "fsdp"), pairs, "both")


def gather_full(links, index, slot, groups):
    columns = yield from along_z(links, slot)
    rows = columns(0, slot.shape[-1])
    got = across(links, rows)
    far = [links.swap(rows, *CORE)]
    yield list(got)
    far += [links.swap(part, *CORE) for part in got]
    yield far
    return assemble(index, [rows, *got, *far], groups)


def gather_halves(links, index, slot, slots):
    columns = yield from along_z(links, slot)
    breadth = slot.shape[-1]
    cut = cut_of(breadth)
    first, second = columns(0, cut), columns(cut, breadth)
    got_first, got_second = links.swap(first, *YAX), links.swap(second, "dp", 1)
    yield [got_first, got_second]
    first = jnp.concatenate([first, got_first], axis=0)
    second = jnp.concatenate([second, got_second], axis=0)
    got_first, got_second = links.swap(first, "dp", 1), links.swap(second, *YAX)
    far_own = [links.swap(first, *CORE), links.swap(second, *CORE)]
    yield [got_first, got_second]
    far_got = [links.swap(got_first, *CORE), links.swap(got_second, *CORE)]
    yield far_own + far_got
    parts = [first, got_first, far_own[0], far_got[0], second, got_second, far_own[1], far_got[1]]
    return assemble_halves(index, parts, [True, False], slots)


def gather_wide(block):
    wide = lax.all_gather(block, "fsdp", axis=2, tiled=True)
    return lax.all_gather(wide, "dp", axis=1, tiled=True)


def gather_dp(links, index, block, z_first):
    if z_first:
        columns = yield from along_z(links, block)
        own = columns(0, block.shape[-1])
        far = links.swap(own, "dp", 1)
        yield [far]
        return place(index, own, far)
    far = links.swap(block, "dp", 1)
    yield [far]
    columns = yield from along_z(links, jnp.stack([block, far]))
    return place(index, columns(0, block.shape[-1]))


class View:
    def __init__(self, base, starts=None, sizes=None):
        self.base = base
        self.starts = starts or [0] * base.ndim
        self.sizes = sizes or list(base.shape)

    def narrow(self, axis, start, size):
        starts, sizes = list(self.starts), list(self.sizes)
        starts[axis] = starts[axis] + start
        sizes[axis] = size
        return View(self.base, starts, sizes)

    def read(self):
        if self.sizes == list(self.base.shape):
            return self.base
        if all(isinstance(start, int) for start in self.starts):
            ends = [start + size for start, size in zip(self.starts, self.sizes)]
            return lax.slice(self.base, self.starts, ends)
        return lax.dynamic_slice(self.base, self.starts, self.sizes)


def total_of(views):
    value = views[0].read().astype(F32)
    for view in views[1:]:
        value = value + view.read().astype(F32)
    return value


def split_on(axis_at):
    return lambda view, bit: view.narrow(axis_at, bit, 1)


def split_rows(axis_at, step, size):
    return lambda view, bit: view.narrow(axis_at, bit * step, size)


def send_half(links, views, axis, mask, choose):
    bit = (lax.axis_index(axis) // mask) % 2
    away = links.hold(1 - bit, (axis, mask))
    send = total_of([choose(view, away) for view in views]).astype(BF16)
    received = links.send(send, axis, xor_pairs(axis, mask), (axis, mask))
    return [choose(view, bit) for view in views], received


def halve(links, views, axis, mask, choose):
    kept, received = send_half(links, views, axis, mask, choose)
    yield [received]
    return kept + [View(received)]


def halve_z(links, views, choose_far, choose_near):
    bit = lax.axis_index("dp") // 4
    away = links.hold(1 - bit, ("dp", 2))
    send = total_of([choose_far(view, away) for view in views]).astype(BF16)
    inward = links.send(send, "dp", INWARD, ("dp", 2))
    yield [inward]
    away = links.hold(1 - bit, "middle")
    send = total_of([choose_far(view, away) for view in views] + [View(inward)]).astype(BF16)
    middle = links.send(send, "dp", MIDDLE, "middle")
    yield [middle]
    views = [choose_far(view, bit) for view in views] + [View(middle)]
    return (yield from halve(links, views, "dp", 2, choose_near))


def reduce_full(links, gradient):
    count, height, breadth = gradient.shape
    rows = height // 8
    slots = Slots(rows)
    by_core = split_rows(4, slots.offset, 2 * slots.size)
    by_y = split_rows(4, slots.size, slots.size)
    by_x = split_on(3)
    views = [View(gradient.reshape(count, 2, 2, 2, rows, breadth))]
    views = yield from halve(links, views, "fsdp", 1, by_core)
    cut = cut_of(breadth)
    first = [view.narrow(5, 0, cut) for view in views]
    second = [view.narrow(5, cut, breadth - cut) for view in views]
    first, got_first = send_half(links, first, "dp", 1, by_x)
    second, got_second = send_half(links, second, "fsdp", 2, by_y)
    yield [got_first, got_second]
    first, second = first + [View(got_first)], second + [View(got_second)]
    first, got_first = send_half(links, first, "fsdp", 2, by_y)
    second, got_second = send_half(links, second, "dp", 1, by_x)
    yield [got_first, got_second]
    first, second = first + [View(got_first)], second + [View(got_second)]
    joined = jnp.concatenate([total_of(first), total_of(second)], axis=-1).astype(BF16)
    views = yield from halve_z(links, [View(joined)], split_on(1), split_on(2))
    return total_of(views).astype(BF16).reshape(count, slots.size, breadth)


def reduce_wide(gradient):
    thin = lax.psum_scatter(gradient.astype(BF16), "fsdp", scatter_dimension=2, tiled=True)
    return lax.psum_scatter(thin.astype(F32), "dp", scatter_dimension=1, tiled=True)


def spread_tokens(rows):
    pair = jnp.concatenate([rows, swap(rows, *YAX)], axis=0)
    return jnp.concatenate([pair, swap(pair, *CORE)], axis=0)


def collect_tokens(partial):
    half = partial.shape[0] // 2
    pair = partial[:half] + swap(partial[half:].astype(BF16), *CORE).astype(F32)
    quarter = half // 2
    return pair[:quarter] + swap(pair[quarter:].astype(BF16), *YAX).astype(F32)


def pick(pair, bit):
    return lax.dynamic_index_in_dim(pair, bit, axis=0, keepdims=False)


def to_latent(pair, y):
    return jnp.concatenate([pick(pair, y), swap(pick(pair, 1 - y), *YAX)], axis=0)


def from_latent(rows, y):
    half = rows.shape[0] // 2
    own = rows[:half]
    other = swap(rows[half:], *YAX)
    return jnp.where(y == 0, jnp.stack([own, other]), jnp.stack([other, own]))


def flatten_all(arrays):
    return jnp.concatenate([matrix.reshape(-1) for matrix in arrays])


def split_all(vector, shapes):
    pieces = []
    offset = 0
    for shape_now in shapes:
        count_now = math.prod(shape_now)
        pieces.append(vector[offset : offset + count_now].reshape(shape_now))
        offset = offset + count_now
    return pieces


def statistics(group, extra, late):
    dp, fsdp = lax.axis_size("dp"), lax.axis_size("fsdp")
    old_sums = jnp.concatenate([jnp.sum(rows, axis=1) for _, _, rows, _ in group])
    master_squares = jnp.concatenate(
        [jnp.sum(after(master, late) ** 2, axis=(1, 2)) for master, _, _, _ in group]
    )
    squares = [gradient * gradient + EPS_SQUARE for _, gradient, _, _ in group]
    row_parts = [jnp.sum(square_block, axis=2) for square_block in squares]
    column_parts = [jnp.sum(square_block, axis=1) for square_block in squares]
    row_sums = split_all(butterfly(flatten_all(row_parts), "fsdp"), [part.shape for part in row_parts])
    over_dp = column_parts + [old_sums / fsdp, master_squares] + ([] if extra is None else [extra])
    over_dp = split_all(butterfly(flatten_all(over_dp), "dp"), [part.shape for part in over_dp])
    column_sums = over_dp[: len(group)]
    totals = [jnp.concatenate([jnp.sum(part, axis=1) for part in column_sums])] + over_dp[len(group) :]
    totals = split_all(butterfly(flatten_all(totals), "fsdp"), [part.shape for part in totals])
    counts = [(part.shape[0],) for part in row_parts]
    square_split, old_split, master_split = [split_all(total, counts) for total in totals[:3]]
    states = []
    for (_, gradient, rows, columns), row_sum, column_sum, square_total, old_total, master_sum in zip(
        group, row_sums, column_sums, square_split, old_split, master_split
    ):
        height, breadth = gradient.shape[1] * dp, gradient.shape[2] * fsdp
        rows_new = DECAY * rows + (1.0 - DECAY) * row_sum / breadth
        columns_new = DECAY * columns + (1.0 - DECAY) * column_sum / height
        mean = (DECAY * old_total + (1.0 - DECAY) * square_total / breadth) / height
        update = gradient * lax.rsqrt(rows_new[:, :, None] * columns_new[:, None, :] / mean[:, None, None])
        states.append((rows_new, columns_new, update, jnp.sum(update * update, axis=(1, 2)), master_sum))
    return states, totals[3] if extra is not None else None


WIDE = 768
MEMBERS = 9


def members_of(arrays):
    return [(at, one, slab.shape[1], slab.shape[2]) for at, slab in enumerate(arrays) for one in range(slab.shape[0])]


def pack_rows(states):
    rows = [jnp.pad(state, ((0, 0), (0, WIDE - state.shape[1]))) for state in states]
    return jnp.pad(jnp.concatenate(rows, axis=0), ((0, 16 - MEMBERS), (0, 0)))


def pack_columns(states):
    rows = [
        jnp.pad(state, ((0, 0), (0, 2 * WIDE - state.shape[1]))).reshape(-1, WIDE) for state in states
    ]
    return jnp.pad(jnp.concatenate(rows, axis=0), ((0, 32 - 2 * MEMBERS), (0, 0)))


def lane_is(index, shape):
    return lax.broadcasted_iota(jnp.int32, shape, 1) == index


def sums_kernel(count, *refs):
    grads, (extra_ref, rows_ref, columns_ref, turn_ref) = refs[:count], refs[count:]
    columns_ref[...] = jnp.zeros(columns_ref.shape, F32)
    turn_ref[...] = jnp.zeros(turn_ref.shape, F32)
    rows_ref[...] = jnp.zeros(rows_ref.shape, F32)
    totals = jnp.zeros((1, WIDE), F32)
    for at, (slab, one, height, breadth) in enumerate(members_of(grads)):
        gradient = grads[slab][one]
        square = gradient * gradient + EPS_SQUARE
        in_row = jnp.sum(square, axis=1, keepdims=True)
        turn_ref[:height, :] += jnp.where(lane_is(at, (height, 128)), in_row, 0.0)
        in_column = jnp.sum(square, axis=0, keepdims=True)
        columns_ref[2 * at : 2 * at + 1, : min(breadth, WIDE)] = in_column[:, :WIDE]
        if breadth > WIDE:
            columns_ref[2 * at + 1 : 2 * at + 2, : breadth - WIDE] = in_column[:, WIDE:]
        totals += jnp.where(lane_is(2 * MEMBERS + at, (1, WIDE)), jnp.sum(in_row), 0.0)
    rows_ref[:16, :] = turn_ref[...].T[:16]
    rows_ref[16:32, :] = extra_ref[...]
    rows_ref[26:27, :] = extra_ref[10:11, :] + totals


def scalar_at(row, index):
    return jnp.sum(jnp.where(lane_is(index, row.shape), row, 0.0))


def updates_of(grads, at, member, turned, columns_ref, mean):
    slab, one, height, breadth = member
    column = columns_ref[2 * at : 2 * at + 1, : min(breadth, WIDE)]
    if breadth > WIDE:
        column = jnp.concatenate([column, columns_ref[2 * at + 1 : 2 * at + 2, : breadth - WIDE]], axis=1)
    row = turned[:height, at : at + 1]
    return grads[slab][one] * lax.rsqrt(row * (column / mean))


def mean_of(scalars, at, height, breadth):
    old, square = scalar_at(scalars, at), scalar_at(scalars, 2 * MEMBERS + at)
    return (DECAY * old + (1.0 - DECAY) * square / breadth) / height


def states_kernel(count, dp, fsdp, *refs):
    grads = refs[:count]
    row_sum_ref, column_sum_ref, old_rows_ref, old_columns_ref = refs[count : count + 4]
    rows_ref, columns_ref, squares_ref, turn_ref = refs[count + 4 :]
    scalars = column_sum_ref[42:43, :]
    rows_ref[...] = jnp.zeros(rows_ref.shape, F32)
    columns_ref[...] = jnp.zeros(columns_ref.shape, F32)
    members = members_of(grads)
    for at, (_, _, height, breadth) in enumerate(members):
        rows_ref[at : at + 1, :] = DECAY * old_rows_ref[at : at + 1, :] + row_sum_ref[at : at + 1, :] * (
            (1.0 - DECAY) / (breadth * fsdp)
        )
        columns_ref[2 * at : 2 * at + 2, :] = DECAY * old_columns_ref[
            2 * at : 2 * at + 2, :
        ] + column_sum_ref[2 * at : 2 * at + 2, :] * ((1.0 - DECAY) / (height * dp))
    turn_ref[:16, :] = rows_ref[...]
    turned = turn_ref[...].T
    found = jnp.zeros((8, 128), F32)
    for at, member in enumerate(members):
        mean = mean_of(scalars, at, member[2] * dp, member[3] * fsdp)
        update = updates_of(grads, at, member, turned, columns_ref, mean)
        found += jnp.where(lane_is(at, (8, 128)), jnp.sum(update * update), 0.0)
    squares_ref[...] = found


def masters_kernel(count, dp, fsdp, *refs):
    grads, masters = refs[:count], refs[count : 2 * count]
    rows_ref, columns_ref, column_sum_ref, squares_ref = refs[2 * count : 2 * count + 4]
    outs, turn_ref = refs[2 * count + 4 : -1], refs[-1]
    scalars = column_sum_ref[42:43, :]
    squares = squares_ref[0:1, :]
    turn_ref[:16, :] = rows_ref[...]
    turned = turn_ref[...].T
    for at, member in enumerate(members_of(grads)):
        slab, one, height, breadth = member
        mean = mean_of(scalars, at, height * dp, breadth * fsdp)
        update = updates_of(grads, at, member, turned, columns_ref, mean)
        entries = height * dp * breadth * fsdp
        row = jnp.zeros((1, 128), F32)
        ratio = jnp.sqrt(row + scalar_at(squares, at) / entries) / CLIP
        scale = jnp.maximum(EPS_SCALE, jnp.sqrt(row + scalar_at(scalars, MEMBERS + at) / entries))
        step = (RATE * scale / jnp.maximum(1.0, ratio))[:, :1]
        outs[slab][one] = masters[slab][one] - step * update


def vmem_call(kernel, operands, shapes, scratch):
    return pl.pallas_call(
        kernel,
        out_shape=[jax.ShapeDtypeStruct(shape, F32) for shape in shapes],
        in_specs=[pl.BlockSpec(memory_space=pltpu.VMEM)] * len(operands),
        out_specs=[pl.BlockSpec(memory_space=pltpu.VMEM)] * len(shapes),
        scratch_shapes=[pltpu.VMEM(shape, F32) for shape in scratch],
        compiler_params=pltpu.CompilerParams(vmem_limit_bytes=40 << 20),
        cost_estimate=pl.CostEstimate(flops=20000000, bytes_accessed=10000000, transcendentals=1200000),
    )(*operands)


def both_axes(value):
    return butterfly(butterfly(value, "fsdp"), "dp")


def fused_update(group, gains_part, late):
    dp, fsdp = lax.axis_size("dp"), lax.axis_size("fsdp")
    masters = [master for master, _, _, _ in group]
    grads = [gradient for _, gradient, _, _ in group]
    rows, columns = [member[2] for member in group], [member[3] for member in group]
    old_sums = jnp.concatenate([jnp.sum(state, axis=1) for state in rows]) / fsdp
    master_squares = jnp.concatenate([jnp.sum(after(master, late) ** 2, axis=(1, 2)) for master in masters])
    scalars = jnp.pad(jnp.concatenate([old_sums, master_squares])[None], ((0, 5), (0, WIDE - 2 * MEMBERS)))
    gains_rows = jnp.pad(gains_part.reshape(10, -1), ((0, 0), (0, WIDE - D // 2)))
    extra = jnp.concatenate([gains_rows, scalars], axis=0)
    old_rows, old_columns = pack_rows(rows), pack_columns(columns)
    count = len(group)
    packed_rows, packed_columns = vmem_call(
        functools.partial(sums_kernel, count), [*grads, extra], [(32, WIDE), (32, WIDE)], [(WIDE, 128)]
    )
    row_sums = butterfly(packed_rows, "fsdp")
    column_sums = butterfly(jnp.concatenate([packed_columns, row_sums[16:]], axis=0), "dp")
    new_rows, new_columns, squares = vmem_call(
        functools.partial(states_kernel, count, dp, fsdp),
        [*grads, row_sums, column_sums, old_rows, old_columns],
        [(16, WIDE), (32, WIDE), (8, 128)],
        [(128, WIDE)],
    )
    squares = both_axes(squares)
    new_masters = vmem_call(
        functools.partial(masters_kernel, count, dp, fsdp),
        [*grads, *masters, new_rows, new_columns, column_sums, squares],
        [master.shape for master in masters],
        [(128, WIDE)],
    )
    finished = []
    at = 0
    for which, (master, gradient, _, _) in enumerate(group):
        many, height, breadth = master.shape
        row_out = new_rows[at : at + many, :height]
        column_out = new_columns[2 * at : 2 * (at + many)].reshape(many, -1)[:, :breadth]
        finished.append([new_masters[which], row_out, column_out, gradient])
        at += many
    gain_total = column_sums[32:42, : D // 2].reshape(5, D)
    return finished, gain_total


def shards(
    latents,
    skip_input,
    text_tokens,
    cotangent,
    timesteps,
    text_lengths,
    positions,
    skip_weight,
    skip_rows,
    skip_columns,
    square_weight,
    square_rows,
    square_columns,
    self_weight,
    self_rows,
    self_columns,
    output_weight,
    output_rows,
    output_columns,
    text_weight,
    text_rows,
    text_columns,
    up_weight,
    up_rows,
    up_columns,
    down_weight,
    down_rows,
    down_columns,
    norm_gains,
    gain_state,
):
    dp = lax.axis_size("dp")
    d_at = lax.axis_index("dp")
    f_at = lax.axis_index("fsdp")
    y_at = f_at // 2
    c_at = f_at % 2
    index = jnp.stack([d_at, f_at]).astype(jnp.int32)

    dp_masks = masks_of("dp")

    fsdp = lax.axis_size("fsdp")
    every = ("dp", "fsdp")
    rows_d = up_weight.shape[0]
    chunk = down_weight.shape[0] // 4
    per_f = up_weight.shape[1] // (4 * chunk)
    quick = fits(rows_d)
    links = Links()
    skip_slots, wide_slots = Slots(skip_weight.shape[0]), Slots(rows_d)
    down_slots = Slots(down_weight.shape[0], True)
    text_slots = Slots(text_weight.shape[0], True)
    skip_block = skip_weight.astype(BF16)[None]
    self_block = self_weight.astype(BF16)[None]
    cross_block = jnp.stack([output_weight[0], square_weight[1], output_weight[1]]).astype(BF16)

    def advance(*flows):
        for flow in flows:
            flow.step()

    text_local = to_latent(text_tokens, y_at)
    places = to_latent(jnp.swapaxes(positions, 1, 2), y_at).T
    text_count = pick(text_lengths, y_at)
    steps = double(timesteps[None], [("dp", mask) for mask in dp_masks])
    rows_q = square_weight.shape[1]
    columns_q = square_weight.shape[2]

    if quick:
        skip_slot = slot_rows(exchange([slot_pieces(skip_block, skip_slots)])[0], skip_slots, 1)
        skip_slot = after(skip_slot, steps, places, text_local)
        skip_flow = Flow(gather_full(links, index, skip_slot, [(0, 1, skip_slots)]))
        skip_flow.step()
        early = skip_flow.pending[0]
    else:
        early = None
    joined = jnp.concatenate([to_latent(latents, y_at), to_latent(skip_input, y_at)], axis=-1).astype(F32)
    shift_block = square_weight[0].astype(BF16)[None]
    if quick:
        self_part, shift_part = after((self_block, shift_block), early)
        got = exchange([slot_pieces(self_part, wide_slots), slot_pieces(shift_part, wide_slots)])
        self_slot = jnp.concatenate([slot_rows(part, wide_slots, 1) for part in got], axis=-1)
        self_flow = Flow(gather_halves(links, index, self_slot, wide_slots))
        advance(skip_flow)
        advance(skip_flow, self_flow)
        advance(skip_flow, self_flow)
        early = skip_flow.pending[0]
    text_part, down_part, up_part, cross_part = after(
        (
            text_weight.astype(BF16)[None],
            down_weight.astype(BF16)[None],
            up_weight.astype(BF16),
            cross_block,
        ),
        early,
    )
    columns_h = per_f * chunk
    up_cuts = [
        [up_part[:, (4 * block + f) * chunk : (4 * block + f + 1) * chunk] for block in range(per_f)]
        for f in range(4)
    ]
    pieces = [
        slot_pieces(down_part, down_slots),
        jnp.stack([jnp.concatenate(cuts, axis=1) for cuts in up_cuts]),
        slot_pieces(text_part, text_slots),
    ]
    if quick:
        pieces.append(slot_pieces(cross_part, wide_slots))
    got = exchange(pieces)
    down_slot = slot_rows(got[0], down_slots, 1)[0]
    up_block = jnp.concatenate([got[1][f] for f in range(4)], axis=1)
    text_slot = slot_rows(got[2], text_slots, 1)
    if quick:
        text_flow = Flow(gather_full(links, index, text_slot, [(0, 1, text_slots)]))
        cross_flow = Flow(gather_halves(links, index, slot_rows(got[3], wide_slots, 3), wide_slots))
        up_flow = Flow(gather_dp(links, index, up_block, True))
        down_flow = Flow(gather_dp(links, index, down_slot, False))
        advance(skip_flow, self_flow)
        advance(self_flow)
    else:
        text_full = lax.all_gather(text_slot[0], every, axis=0, tiled=True)
        down_full = lax.all_gather(down_slot, "dp", axis=0, tiled=True)
    embed_own = jax.nn.silu(time_embed(pick(timesteps, y_at)[None], D)).astype(BF16)

    if quick:
        skip_full = skip_flow.finish()[0][0]
    else:
        skip_full = gather_wide(skip_block)[0]

    normed_skip, pull_skip = jax.vjp(skip_norm, joined, norm_gains[0:2].reshape(-1))
    lowered_skip = normed_skip.astype(BF16)
    stream = matmul(lowered_skip, skip_full)
    links.gate = stream
    if quick:
        advance(self_flow)
        links.gate = stream
        advance(text_flow, cross_flow)
        advance(text_flow, cross_flow, up_flow)
        both_full = self_flow.finish()[0]
        self_full, shift_full = both_full[:, : 3 * D], both_full[:, 3 * D :]
    else:
        self_full, shift_full = gather_wide(self_block)[0], gather_wide(shift_block)[0]
    shift_row = matmul(embed_own, shift_full)
    normed_self, pull_self_norm = jax.vjp(modulated, stream, norm_gains[2], shift_row)
    lowered_self = normed_self.astype(BF16)
    joint = matmul(lowered_self, self_full)
    links.gate = joint
    if quick:
        links.gate = joint
        advance(text_flow, cross_flow, up_flow)
        advance(text_flow, cross_flow, up_flow, down_flow)
        advance(text_flow, cross_flow, down_flow)

    def prepare(linear):
        return head_prep(linear, places)

    query_rows, pull_query = jax.vjp(prepare, joint[:, :D])
    key_local, pull_key = jax.vjp(prepare, joint[:, D : 2 * D])
    queries = query_rows.astype(BF16)
    key_value = jnp.stack([key_local.astype(BF16), joint[:, 2 * D :].astype(BF16)])
    key_value = jnp.concatenate([key_value, swap(key_value, *CORE)], axis=1)
    key_all, value_all = key_value[0], key_value[1]

    upstream = to_latent(after(cotangent, stream), y_at)
    upstream_pair = jnp.concatenate([upstream, swap(upstream, *YAX)], axis=0)
    upstream_far = swap(upstream_pair, *CORE)
    upstream_all = jnp.concatenate([upstream_pair, upstream_far], axis=0)
    attended, self_logsum = attend_forward(queries, key_all, value_all, None)
    attended = after(attended, upstream_far)
    links.gate = attended
    if quick:
        text_full = text_flow.finish()[0][0]
        advance(up_flow, cross_flow, down_flow)
        cross_full = cross_flow.finish()
    else:
        cross_full = gather_wide(cross_block)
    text_joint = matmul(text_local, text_full)
    text_key_local, pull_text_key = jax.vjp(head_norm, text_joint[:, :D])
    text_kv = jnp.stack([text_key_local.astype(BF16), text_joint[:, D:].astype(BF16)])
    text_kv = jnp.concatenate([text_kv, swap(text_kv, *CORE)], axis=1)
    text_key_all, text_value_all = text_kv[0], text_kv[1]

    out_self, square_cross, out_cross = cross_full[0], cross_full[1], cross_full[2]
    self_stream = stream + matmul(attended, out_self)
    normed_cross, pull_cross_norm = jax.vjp(gained, self_stream, norm_gains[3])
    lowered_cross = normed_cross.astype(BF16)
    cross_linear = matmul(lowered_cross, square_cross)
    cross_query_rows, pull_cross_query = jax.vjp(prepare, cross_linear)
    cross_queries = cross_query_rows.astype(BF16)
    own_text = text_tokens.shape[1]
    text_places = jnp.concatenate(
        [(f_at ^ mask) * own_text + jnp.arange(own_text) for mask in (0, 2, 1, 3)]
    )
    valid_keys = text_places < text_count
    cross_attended, cross_logsum = attend_forward(cross_queries, text_key_all, text_value_all, valid_keys)
    cross_stream = self_stream + matmul(cross_attended, out_cross)
    normed_mlp, pull_mlp_norm = jax.vjp(gained, cross_stream, norm_gains[4])
    lowered_mlp = spread_tokens(normed_mlp.astype(BF16))
    if quick:
        up_full = up_flow.finish().reshape(dp * rows_d, -1)
        down_full = down_flow.finish().reshape(dp * chunk, D)
    else:
        up_full = lax.all_gather(up_block, "dp", axis=0, tiled=True)
    hidden_pre = matmul(lowered_mlp, up_full)
    hidden_rows, pull_gelu = jax.vjp(gelu_tanh, hidden_pre)
    hidden_low = hidden_rows.astype(BF16)
    block_partial = matmul(hidden_low, down_full)

    back = Links()

    grad_hidden = matmul_right(upstream_all, down_full)
    grad_pre = pull_gelu(grad_hidden)[0].astype(BF16)
    mlp_partial = matmul_right(grad_pre, up_full)
    term_down = matmul_left(hidden_low, upstream_all).astype(BF16)
    down_rows_sum = lax.psum_scatter(term_down, "dp", scatter_dimension=0, tiled=True)
    term_up = matmul_left(lowered_mlp, grad_pre).astype(BF16)
    up_rows_sum = lax.psum_scatter(term_up, "dp", scatter_dimension=0, tiled=True)
    grad_mlp_in = after(collect_tokens(mlp_partial), term_down, term_up)
    block_rows = (cross_stream + collect_tokens(after(block_partial, grad_mlp_in))).astype(BF16)
    block_output = from_latent(block_rows, y_at)

    grad_cross_part, grad_gain_mlp = pull_mlp_norm(grad_mlp_in)
    grad_cross_stream = upstream.astype(F32) + grad_cross_part
    cross_low = grad_cross_stream.astype(BF16)
    grad_cross_att = matmul_right(cross_low, out_cross).astype(BF16)
    grad_cross_q, grad_text_key, grad_text_value = attend_backward(
        cross_queries, text_key_all, text_value_all, valid_keys, cross_logsum, grad_cross_att
    )
    grad_text_kv = jnp.stack([grad_text_key, grad_text_value])
    text_half = grad_text_kv.shape[1] // 2
    grad_text_got = swap(grad_text_kv[:, text_half:].astype(BF16), *CORE)
    grad_cross_linear = pull_cross_query(grad_cross_q)[0].astype(BF16)
    grad_cross_in = matmul_right(grad_cross_linear, square_cross)
    grad_self_part, grad_gain_cross = pull_cross_norm(grad_cross_in)
    grad_self_stream = grad_cross_stream + grad_self_part
    self_low = grad_self_stream.astype(BF16)
    grad_self_att = matmul_right(self_low, out_self).astype(BF16)
    cross_terms = lax.dot_general(
        jnp.stack([attended, lowered_cross, cross_attended]),
        jnp.stack([self_low, grad_cross_linear, cross_low]),
        (((1,), (1,)), ((0,), (0,))),
        preferred_element_type=F32,
    ).astype(BF16)
    if quick:
        cross_back = Flow(reduce_full(back, cross_terms))
        cross_back.step()
    grad_query, grad_key_all, grad_value_all = attend_backward(
        queries, key_all, value_all, None, self_logsum, grad_self_att
    )
    grad_kv = jnp.stack([grad_key_all, grad_value_all])
    token_half = grad_kv.shape[1] // 2
    grad_kv_got = swap(grad_kv[:, token_half:].astype(BF16), *CORE)

    grad_text_local = grad_text_kv[:, :text_half] + grad_text_got.astype(F32)
    text_grad_joint = jnp.concatenate(
        [pull_text_key(grad_text_local[0])[0], grad_text_local[1]], axis=-1
    ).astype(BF16)
    term_text = matmul_left(text_local, text_grad_joint).astype(BF16)
    text_rows_sum = lax.psum_scatter(after(term_text, term_up), every, scatter_dimension=0, tiled=True)

    grad_kv_local = grad_kv[:, :token_half] + grad_kv_got.astype(F32)
    grad_joint = jnp.concatenate(
        [pull_query(grad_query)[0], pull_key(grad_kv_local[0])[0], grad_kv_local[1]], axis=-1
    ).astype(BF16)
    term_self = matmul_left(lowered_self, grad_joint).astype(BF16)[None]
    if quick:
        back.gate = term_self
        cross_back.step()
        self_back = Flow(reduce_full(back, term_self))
        self_back.step()
    grad_self_in = matmul_right(grad_joint, self_full)
    grad_stream_part, grad_gain_self, grad_shift = pull_self_norm(grad_self_in)
    grad_stream = grad_self_stream + grad_stream_part
    stream_low = grad_stream.astype(BF16)
    term_skip = matmul_left(lowered_skip, stream_low).astype(BF16)[None]
    if quick:
        back.gate = term_skip
        skip_back = Flow(reduce_full(back, term_skip))
        skip_back.step()
    grad_skip_in = matmul_right(stream_low, skip_full)
    if quick:
        back.gate = grad_skip_in
        advance(cross_back, self_back, cross_back, self_back, skip_back, cross_back, skip_back)
    grad_joined, grad_gain_skip = pull_skip(grad_skip_in)
    first_pieces = [
        back_pieces(text_rows_sum.astype(BF16)[None]),
        back_pieces(down_rows_sum.astype(BF16)[None]),
        jnp.swapaxes(up_rows_sum.astype(BF16).reshape(rows_d, 4, per_f * chunk), 0, 1),
    ]
    if quick:
        first_pieces.append(back_pieces(cross_back.finish()))
    latents_grad = from_latent(grad_joined[:, :D].astype(BF16), y_at)
    skip_input_grad = from_latent(grad_joined[:, D:].astype(BF16), y_at)

    quiet = None
    if quick:
        advance(self_back, skip_back, self_back, skip_back)
        quiet = skip_back.pending[0]
        last_pieces = [back_pieces(self_back.finish()), back_pieces(skip_back.finish())]
        first_pieces += last_pieces
    got = exchange(first_pieces, quiet)
    text_sum = back_block(got[0], text_slots, 1).astype(F32)
    down_sum = back_block(got[1], down_slots, 1).astype(F32)
    up_cuts = [
        got[2][f][:, block * chunk : (block + 1) * chunk] for block in range(per_f) for f in range(4)
    ]
    up_sum = jnp.concatenate(up_cuts, axis=1).astype(F32)[None]
    if quick:
        cross_sum = back_block(got[3], wide_slots, 3).astype(F32)
    else:
        cross_sum = reduce_wide(cross_terms)

    embed_all = jax.nn.silu(time_embed(steps.reshape(-1), D)).astype(BF16)
    embed_part = lax.dynamic_slice_in_dim(embed_all, d_at * rows_q, rows_q, axis=1)
    grad_shift = after(grad_shift.reshape(1, D), quiet)
    grad_shift = grad_shift + swap(grad_shift, *CORE)
    other_shift = swap(grad_shift, *YAX)
    shift_pair = jnp.where(
        y_at == 0,
        jnp.concatenate([grad_shift, other_shift]),
        jnp.concatenate([other_shift, grad_shift]),
    )
    shift_pair = lax.dynamic_slice_in_dim(shift_pair, f_at * columns_q, columns_q, axis=1)
    shift_grads = double(shift_pair[None], [("dp", mask) for mask in dp_masks]).reshape(-1, columns_q)
    modulate_sum = lax.dot_general(
        embed_part.astype(F32),
        shift_grads,
        (((0,), (0,)), ((), ())),
        precision=lax.Precision.HIGHEST,
        preferred_element_type=F32,
    )

    gains_part = jnp.concatenate(
        [grad_gain_skip.reshape(2, -1), grad_gain_self[None], grad_gain_cross[None], grad_gain_mlp[None]],
        axis=0,
    )
    square_sum = jnp.stack([modulate_sum, cross_sum[1]])
    output_sum = jnp.stack([cross_sum[0], cross_sum[2]])
    early_group = [
        (square_weight, square_sum, square_rows, square_columns),
        (output_weight, output_sum, output_rows, output_columns),
        (text_weight[None], text_sum, text_rows[None], text_columns[None]),
        (up_weight[None], up_sum, up_rows[None], up_columns[None]),
        (down_weight[None], down_sum, down_rows[None], down_columns[None]),
    ]
    if quick:
        self_sum = back_block(got[4], wide_slots, 1).astype(F32)
        skip_sum = back_block(got[5], skip_slots, 1).astype(F32)
    else:
        self_sum, skip_sum = reduce_wide(term_self), reduce_wide(term_skip)
    late_group = [
        (skip_weight[None], skip_sum, skip_rows[None], skip_columns[None]),
        (self_weight[None], self_sum, self_rows[None], self_columns[None]),
    ]
    groups = late_group + early_group
    if quick:
        finished, gain_total = fused_update(groups, gains_part, joint)
    else:
        states, gain_total = statistics(groups, gains_part, joint)
        update_squares = jnp.concatenate([state[3] for state in states])
        update_all = butterfly(butterfly(update_squares, "fsdp"), "dp")
        update_split = split_all(update_all, [state[3].shape for state in states])
        finished = []
        for (master, gradient, _, _), state, update_sum in zip(groups, states, update_split):
            rows_new, columns_new, update, _, master_sum = state
            entries = gradient.shape[1] * dp * gradient.shape[2] * fsdp
            ratio = jnp.sqrt(update_sum / entries) / CLIP
            step_scale = jnp.maximum(EPS_SCALE, jnp.sqrt(master_sum / entries))
            master_new = master - (RATE * step_scale / jnp.maximum(1.0, ratio))[:, None, None] * update
            finished.append([master_new, rows_new, columns_new, gradient])
    skip_done, self_done, square_done, output_done, text_done, up_done, down_done = finished
    gain_state_new = DECAY * gain_state + (1.0 - DECAY) * (gain_total * gain_total + EPS_SQUARE)
    gain_update = gain_total * lax.rsqrt(gain_state_new)
    gain_ratio = jnp.sqrt(jnp.mean(gain_update * gain_update)) / CLIP
    gain_scale = jnp.maximum(EPS_SCALE, jnp.sqrt(jnp.mean(norm_gains * norm_gains)))
    gains_new = norm_gains - RATE * gain_scale * gain_update / jnp.maximum(1.0, gain_ratio)
    results = [block_output, latents_grad, skip_input_grad]
    for which, group in enumerate(
        [skip_done, square_done, self_done, output_done, text_done, up_done, down_done]
    ):
        if which in (1, 3):
            results.extend(group)
        else:
            results.extend(item[0] for item in group)
    return tuple(results) + (gains_new, gain_state_new, gain_total)


def solution(mesh):
    matrix, row, column = P("dp", "fsdp"), P("dp"), P("fsdp")
    pair, pair_row, pair_column = P(None, "dp", "fsdp"), P(None, "dp"), P(None, "fsdp")
    tokens = P("dp", "fsdp", None)
    kinds = (False, True, False, True, False, False, False)
    in_specs = [tokens] * 4 + [P("dp"), P("dp"), P("dp", None, "fsdp")]
    out_specs = [tokens] * 3
    for paired in kinds:
        if paired:
            in_specs += [pair, pair_row, pair_column]
            out_specs += [pair, pair_row, pair_column, pair]
        else:
            in_specs += [matrix, row, column]
            out_specs += [matrix, row, column, matrix]
    return jax.shard_map(
        shards,
        mesh=mesh,
        in_specs=tuple(in_specs + [P(), P()]),
        out_specs=tuple(out_specs + [P(), P(), P()]),
        check_vma=False,
    )
```

```python
import functools
import math

import jax
import jax.numpy as jnp
from jax import lax
from jax.experimental import pallas as pl
from jax.experimental.pallas import tpu as pltpu
from jax.sharding import PartitionSpec as P

D = 1408
HEADS = 16

EPS_NORM = 1e-06
EPS_SQUARE = 1e-30
EPS_SCALE = 0.001
DECAY = 0.5
CLIP = 1.0
RATE = 0.5

BF16 = jnp.bfloat16
F32 = jnp.float32


def matmul(left, right):
    return jnp.dot(left, right, preferred_element_type=F32)


def matmul_left(left, right):
    return lax.dot_general(left, right, (((0,), (0,)), ((), ())), preferred_element_type=F32)


def matmul_right(left, right):
    return lax.dot_general(left, right, (((1,), (1,)), ((), ())), preferred_element_type=F32)


def norm_rows(values):
    center = values - jnp.mean(values, axis=-1, keepdims=True)
    spread = jnp.mean(center * center, axis=-1, keepdims=True)
    return center * lax.rsqrt(spread + EPS_NORM)


def rotary(values, places):
    half_width = values.shape[-1] // 2
    quarter = half_width // 2
    frequency = jnp.exp(-math.log(10000.0) * jnp.arange(quarter).astype(F32) / quarter)
    pieces = []
    for member in range(2):
        block = values[..., member * half_width : (member + 1) * half_width]
        angles = places[member].astype(F32)[:, None] * frequency[None, :]
        cosine = jnp.cos(angles)[:, None, :]
        sine = jnp.sin(angles)[:, None, :]
        former = block[..., :quarter]
        latter = block[..., quarter:]
        pieces.append(former * cosine - latter * sine)
        pieces.append(latter * cosine + former * sine)
    return jnp.concatenate(pieces, axis=-1)


def time_embed(steps, model_width):
    half_width = model_width // 2
    frequency = jnp.exp(-math.log(10000.0) * jnp.arange(half_width).astype(F32) / half_width)
    angles = steps.astype(F32)[:, None] * frequency[None, :]
    return jnp.concatenate([jnp.cos(angles), jnp.sin(angles)], axis=-1)


def skip_norm(joined, gain_skip):
    return norm_rows(joined) * gain_skip


def modulated(stream, gain_row, shift_row):
    return norm_rows(stream) * gain_row + shift_row


def gained(stream, gain_row):
    return norm_rows(stream) * gain_row


def head_prep(linear, places):
    row_count = linear.shape[0]
    shaped = linear.reshape(row_count, HEADS, -1)
    return rotary(norm_rows(shaped), places).reshape(row_count, -1)


def head_norm(linear):
    row_count = linear.shape[0]
    return norm_rows(linear.reshape(row_count, HEADS, -1)).reshape(row_count, -1)


def gelu_tanh(values):
    return jax.nn.gelu(values, approximate=True)


def attend_scores(queries, key_rows, valid_keys):
    query_count = queries.shape[0]
    head_size = queries.shape[1] // HEADS
    shaped_query = queries.reshape(query_count, HEADS, head_size)
    shaped_keys = key_rows.reshape(key_rows.shape[0], HEADS, head_size)
    score_scale = 1.0 / math.sqrt(head_size)
    scores = jnp.einsum("qhd,khd->hqk", shaped_query, shaped_keys, preferred_element_type=F32) * score_scale
    if valid_keys is not None:
        scores = jnp.where(valid_keys[None, None, :], scores, -1e30)
    return scores, shaped_query, shaped_keys, score_scale


def attend_forward(queries, key_rows, value_rows, valid_keys):
    query_count = queries.shape[0]
    scores, _, _, _ = attend_scores(queries, key_rows, valid_keys)
    shaped_values = value_rows.reshape(value_rows.shape[0], HEADS, -1)
    row_top = jnp.max(scores, axis=-1, keepdims=True)
    logsum = row_top + jnp.log(jnp.sum(jnp.exp(scores - row_top), axis=-1, keepdims=True))
    weights_soft = jnp.exp(scores - logsum).astype(BF16)
    mixture = jnp.einsum("hqk,khd->qhd", weights_soft, shaped_values, preferred_element_type=F32)
    return mixture.reshape(query_count, -1).astype(BF16), logsum


def attend_backward(queries, key_rows, value_rows, valid_keys, logsum, grad_mixture):
    query_count = queries.shape[0]
    scores, shaped_query, shaped_keys, score_scale = attend_scores(queries, key_rows, valid_keys)
    shaped_values = value_rows.reshape(value_rows.shape[0], HEADS, -1)
    shaped_grad = grad_mixture.reshape(query_count, HEADS, -1)
    weights_full = jnp.exp(scores - logsum)
    weights_soft = weights_full.astype(BF16)
    grad_weights = jnp.einsum("qhd,khd->hqk", shaped_grad, shaped_values, preferred_element_type=F32)
    grad_values = jnp.einsum("hqk,qhd->khd", weights_soft, shaped_grad, preferred_element_type=F32)
    row_delta = jnp.sum(weights_full * grad_weights, axis=-1, keepdims=True)
    grad_scores = (weights_full * (grad_weights - row_delta)).astype(BF16)
    grad_queries = (
        jnp.einsum("hqk,khd->qhd", grad_scores, shaped_keys, preferred_element_type=F32) * score_scale
    )
    grad_keys = (
        jnp.einsum("hqk,qhd->khd", grad_scores, shaped_query, preferred_element_type=F32) * score_scale
    )
    key_count = key_rows.shape[0]
    return (
        grad_queries.reshape(query_count, -1),
        grad_keys.reshape(key_count, -1),
        grad_values.reshape(key_count, -1),
    )


def swap(value, axis, mask):
    size = lax.axis_size(axis)
    return lax.ppermute(value, axis, [(i, i ^ mask) for i in range(size)])


def masks_of(axis):
    size = lax.axis_size(axis)
    return [1 << b for b in range(size.bit_length() - 1)]


def butterfly(value, axis):
    for mask in masks_of(axis):
        value = value + swap(value, axis, mask)
    return value


def after(value, *others):
    others = [other for other in others if other is not None]
    if not others:
        return value
    return lax.optimization_barrier((value, *others))[0]


class Links:
    def __init__(self, depth=2):
        self.depth = depth
        self.sent = {}
        self.gate = None

    def hold(self, value, link):
        queue = self.sent.setdefault(link, [])
        earlier = queue[-self.depth] if len(queue) >= self.depth else None
        return after(value, earlier, self.gate)

    def send(self, value, axis, pairs, link):
        got = lax.ppermute(value, axis, pairs)
        self.sent.setdefault(link, []).append(got)
        return got

    def move(self, value, axis, pairs, link):
        return self.send(self.hold(value, link), axis, pairs, link)

    def swap(self, value, axis, mask):
        return self.move(value, axis, xor_pairs(axis, mask), (axis, mask))


def xor_pairs(axis, mask):
    return [(i, i ^ mask) for i in range(lax.axis_size(axis))]


class Flow:
    def __init__(self, stages):
        self.stages = stages
        self.pending = []
        self.result = None

    def step(self, main=None):
        if self.result is not None:
            return main
        if main is not None:
            main = after(main, *self.pending)
        try:
            self.pending = next(self.stages)
        except StopIteration as end:
            self.pending = []
            self.result = end.value
        return main

    def finish(self):
        while self.result is None:
            self.step()
        return self.result


MIDDLE = [(2, 4), (3, 5), (4, 2), (5, 3)]
OUTWARD = [(2, 0), (3, 1), (4, 6), (5, 7)]
INWARD = [(0, 2), (1, 3), (6, 4), (7, 5)]


CORE = ("fsdp", 1)
YAX = ("fsdp", 2)


class Slots:
    def __init__(self, rows, plain=False, size=None):
        self.rows = rows
        self.plain = plain
        self.size = rows // 4 if plain else size or -(-rows // 64) * 16
        self.offset = rows - 2 * self.size
        self.overlap = 4 * self.size - rows

    def skip(self, index):
        if self.plain or index % 2 == 0:
            return 0
        return min(self.size, max(0, 2 * self.size - self.start(index)))

    def start(self, index):
        if self.plain:
            return index * self.size
        return (index % 2) * self.offset + (index // 2) * self.size


def exchange(pieces, gate=None):
    widest = max(piece.shape[2] for piece in pieces)
    joined = jnp.concatenate(
        [jnp.pad(piece, ((0, 0), (0, 0), (0, widest - piece.shape[2]))) for piece in pieces], axis=1
    )
    got = lax.all_to_all(after(joined, gate), "fsdp", 0, 0, tiled=False)
    made = []
    offset = 0
    for piece in pieces:
        made.append(got[:, offset : offset + piece.shape[1], : piece.shape[2]])
        offset += piece.shape[1]
    return made


def slot_pieces(block, slots):
    count, _, breadth = block.shape
    chunk = D // 4
    cuts = jnp.stack(
        [lax.slice_in_dim(block, slots.start(f), slots.start(f) + slots.size, axis=1) for f in range(4)]
    )
    cuts = cuts.reshape(4, count, slots.size, breadth // chunk, chunk)
    return jnp.swapaxes(cuts, 2, 3).reshape(4, -1, chunk)


def slot_rows(got, slots, count):
    chunk = got.shape[2]
    shaped = got.reshape(4, count, -1, slots.size, chunk)
    return jnp.transpose(shaped, (1, 3, 0, 2, 4)).reshape(count, slots.size, -1)


def back_pieces(rows):
    count, size, breadth = rows.shape
    chunk = D // 4
    shaped = rows.reshape(count, size, 4, breadth // (4 * chunk), chunk)
    return jnp.transpose(shaped, (2, 0, 3, 1, 4)).reshape(4, -1, chunk)


def back_block(got, slots, count):
    chunk = got.shape[2]
    shaped = jnp.swapaxes(got.reshape(4, count, -1, slots.size, chunk), 2, 3)
    shaped = shaped.reshape(4, count, slots.size, -1)
    if slots.plain:
        return jnp.swapaxes(shaped, 0, 1).reshape(count, slots.rows, -1)
    return jnp.concatenate(
        [shaped[0], shaped[2], shaped[1][:, slots.overlap :], shaped[3]], axis=1
    )


def staged(pairs, in_sems, out_sems):
    arrivals = [
        pltpu.make_async_copy(source, hold, in_sems.at[k]) for k, (source, hold, _, _) in enumerate(pairs)
    ]
    for copy in arrivals:
        copy.start()
    departures = []
    for k, (_, _, held, target) in enumerate(pairs):
        arrivals[k].wait()
        copy = pltpu.make_async_copy(held, target, out_sems.at[k])
        copy.start()
        departures.append(copy)
    for copy in departures:
        copy.wait()


def z_sources(z_at):
    return [z_at, z_at ^ 1, jnp.where(z_at < 2, 2, 1), jnp.where(z_at < 2, 3, 0)]


def assemble_kernel(groups, index_ref, *refs):
    here_z = index_ref[0] // 2
    here_x = index_ref[0] % 2
    here_f = index_ref[1]
    out_refs = refs[8 : 8 + len(groups)]
    hold_ref, in_sems, out_sems = refs[8 + len(groups) :]
    sources = z_sources(here_z)

    def copies(f):
        arrivals, departures = [], []
        for side in range(8):
            source_f = f ^ (side // 4) ^ (side & 2)
            for k in range(4):
                source_dp = 2 * sources[k] + (here_x ^ (side & 1))
                at = side * 4 + k
                arrivals.append(pltpu.make_async_copy(refs[side].at[k], hold_ref.at[at], in_sems.at[at]))
                leaving = []
                for which, (first, count, slots) in enumerate(groups):
                    skip = slots.skip(source_f)
                    if skip == slots.size:
                        continue
                    row = source_dp * slots.rows + slots.start(source_f) + skip
                    row = pl.multiple_of(row, 16)
                    size = slots.size - skip
                    leaving.append(
                        pltpu.make_async_copy(
                            hold_ref.at[at, pl.ds(first, count), pl.ds(skip, size), :],
                            out_refs[which].at[:, pl.ds(row, size), :],
                            out_sems.at[at * len(groups) + which],
                        )
                    )
                departures.append(leaving)
        return arrivals, departures

    for f in range(4):

        @pl.when(here_f == f)
        def _():
            arrivals, departures = copies(f)
            for copy in arrivals:
                copy.start()
            for copy, leaving in zip(arrivals, departures):
                copy.wait()
                for onward in leaving:
                    onward.start()
            for leaving in departures:
                for onward in leaving:
                    onward.wait()


def assemble(index, parts, groups):
    _, total, size, breadth = parts[0].shape
    return pl.pallas_call(
        functools.partial(assemble_kernel, groups),
        out_shape=[
            jax.ShapeDtypeStruct((count, 8 * slots.rows, breadth), BF16) for _, count, slots in groups
        ],
        in_specs=[pl.BlockSpec(memory_space=pltpu.SMEM)] + [pl.BlockSpec(memory_space=pl.ANY)] * 8,
        out_specs=[pl.BlockSpec(memory_space=pl.ANY)] * len(groups),
        scratch_shapes=[
            pltpu.VMEM((32, total, size, breadth), BF16),
            pltpu.SemaphoreType.DMA((32,)),
            pltpu.SemaphoreType.DMA((32 * len(groups),)),
        ],
        compiler_params=pltpu.CompilerParams(vmem_limit_bytes=32 << 20),
        cost_estimate=pl.CostEstimate(
            flops=0, bytes_accessed=128 * total * size * breadth, transcendentals=0
        ),
    )(index, *parts)


def assemble_halves_kernel(orders, slots, index_ref, *refs):
    here_z = index_ref[0] // 2
    here_x = index_ref[0] % 2
    here_f = index_ref[1]
    count = len(orders)
    part_refs, out_ref = refs[: 4 * count], refs[4 * count]
    holds, (in_sems, out_sems) = refs[4 * count + 1 : 5 * count + 1], refs[5 * count + 1 :]
    sources = z_sources(here_z)

    def pairs(f):
        made = []
        left = 0
        for which, y_first in enumerate(orders):
            width = part_refs[4 * which].shape[-1]
            for side in range(4):
                ref = part_refs[4 * which + side]
                for k in range(8):
                    bits = (k // 4, side % 2)
                    y_bit, x_bit = bits if y_first else bits[::-1]
                    source_f = f ^ (side // 2) ^ (2 * y_bit)
                    source_dp = 2 * sources[k % 4] + (here_x ^ x_bit)
                    skip = slots.skip(source_f)
                    row = source_dp * slots.rows + slots.start(source_f) + skip
                    row = pl.multiple_of(row, 16)
                    size = slots.size - skip
                    hold = holds[which].at[side * 8 + k]
                    made.append(
                        (
                            ref.at[k],
                            hold,
                            holds[which].at[side * 8 + k, :, pl.ds(skip, size), :],
                            out_ref.at[:, pl.ds(row, size), pl.ds(left, width)],
                        )
                    )
            left += width
        return made

    for f in range(4):

        @pl.when(here_f == f)
        def _():
            staged(pairs(f), in_sems, out_sems)


def assemble_halves(index, parts, orders, slots):
    count, size = parts[0].shape[1:3]
    total = lax.axis_size("dp") * slots.rows
    breadth = sum(part.shape[-1] for part in parts[::4])
    bytes_now = 2 * count * total * breadth
    copies = 32 * len(orders)
    return pl.pallas_call(
        functools.partial(assemble_halves_kernel, orders, slots),
        out_shape=jax.ShapeDtypeStruct((count, total, breadth), BF16),
        in_specs=[pl.BlockSpec(memory_space=pltpu.SMEM)] + [pl.BlockSpec(memory_space=pl.ANY)] * len(parts),
        out_specs=pl.BlockSpec(memory_space=pl.ANY),
        scratch_shapes=[pltpu.VMEM((32, count, size, part.shape[-1]), BF16) for part in parts[::4]]
        + [pltpu.SemaphoreType.DMA((copies,)), pltpu.SemaphoreType.DMA((copies,))],
        compiler_params=pltpu.CompilerParams(vmem_limit_bytes=24 << 20),
        cost_estimate=pl.CostEstimate(flops=0, bytes_accessed=2 * bytes_now, transcendentals=0),
    )(index, *parts)


def place_kernel(index_ref, *refs):
    parts, (out_ref, hold_ref, in_sems, out_sems) = refs[:-4], refs[-4:]
    sources = z_sources(index_ref[0] // 2)
    here_x = index_ref[0] % 2
    made = []
    for side in range(2):
        for k in range(4):
            hold = hold_ref.at[k + side * 4]
            source = parts[side].at[k] if len(parts) == 2 else parts[0].at[k, side]
            made.append((source, hold, hold, out_ref.at[2 * sources[k] + (here_x ^ side)]))
    staged(made, in_sems, out_sems)


def place(index, *parts):
    rows, breadth = parts[0].shape[-2:]
    return pl.pallas_call(
        place_kernel,
        out_shape=jax.ShapeDtypeStruct((8, rows, breadth), BF16),
        in_specs=[pl.BlockSpec(memory_space=pltpu.SMEM)] + [pl.BlockSpec(memory_space=pl.ANY)] * len(parts),
        out_specs=pl.BlockSpec(memory_space=pl.ANY),
        scratch_shapes=[
            pltpu.VMEM((8, rows, breadth), BF16),
            pltpu.SemaphoreType.DMA((8,)),
            pltpu.SemaphoreType.DMA((8,)),
        ],
        compiler_params=pltpu.CompilerParams(vmem_limit_bytes=24 << 20),
        cost_estimate=pl.CostEstimate(flops=0, bytes_accessed=32 * rows * breadth, transcendentals=0),
    )(index, *parts)


def double(buffer, stages):
    for axis, mask in stages:
        buffer = jnp.concatenate([buffer, swap(buffer, axis, mask)], axis=0)
    return buffer


def fits(rows):
    return lax.axis_size("dp") == 8 and rows % 16 == 0 and rows >= 64


def along_z(links, buffer):
    got = links.swap(buffer, "dp", 2)
    yield [got]
    pair = jnp.stack([buffer, got])
    middle = links.move(pair, "dp", MIDDLE, "middle")
    yield [middle]
    outer = links.move(middle, "dp", OUTWARD, ("dp", 2))
    yield [outer]
    z_at = lax.axis_index("dp") // 2
    inner = (z_at == 1) | (z_at == 2)

    def columns(first, last):
        far = jnp.where(inner, middle[..., first:last], outer[..., first:last])
        return jnp.concatenate([pair[..., first:last], far], axis=0)

    return columns


def cut_of(breadth):
    return (breadth // 128 + 1) // 2 * 128


def across(links, value):
    pairs = [(i, i ^ 6) for i in range(4 * lax.axis_size("dp"))]
    got_x, got_y = links.swap(value, "dp", 1), links.swap(value, *YAX)
    return got_x, got_y, links.move(value, ("dp", "fsdp"), pairs, "both")


def gather_full(links, index, slot, groups):
    columns = yield from along_z(links, slot)
    rows = columns(0, slot.shape[-1])
    got = across(links, rows)
    far = [links.swap(rows, *CORE)]
    yield list(got)
    far += [links.swap(part, *CORE) for part in got]
    yield far
    return assemble(index, [rows, *got, *far], groups)


def gather_halves(links, index, slot, slots):
    columns = yield from along_z(links, slot)
    breadth = slot.shape[-1]
    cut = cut_of(breadth)
    first, second = columns(0, cut), columns(cut, breadth)
    got_first, got_second = links.swap(first, *YAX), links.swap(second, "dp", 1)
    yield [got_first, got_second]
    first = jnp.concatenate([first, got_first], axis=0)
    second = jnp.concatenate([second, got_second], axis=0)
    got_first, got_second = links.swap(first, "dp", 1), links.swap(second, *YAX)
    far_own = [links.swap(first, *CORE), links.swap(second, *CORE)]
    yield [got_first, got_second]
    far_got = [links.swap(got_first, *CORE), links.swap(got_second, *CORE)]
    yield far_own + far_got
    parts = [first, got_first, far_own[0], far_got[0], second, got_second, far_own[1], far_got[1]]
    return assemble_halves(index, parts, [True, False], slots)


def gather_wide(block):
    wide = lax.all_gather(block, "fsdp", axis=2, tiled=True)
    return lax.all_gather(wide, "dp", axis=1, tiled=True)


def gather_dp(links, index, block, z_first):
    if z_first:
        columns = yield from along_z(links, block)
        own = columns(0, block.shape[-1])
        far = links.swap(own, "dp", 1)
        yield [far]
        return place(index, own, far)
    far = links.swap(block, "dp", 1)
    yield [far]
    columns = yield from along_z(links, jnp.stack([block, far]))
    return place(index, columns(0, block.shape[-1]))


class View:
    def __init__(self, base, starts=None, sizes=None):
        self.base = base
        self.starts = starts or [0] * base.ndim
        self.sizes = sizes or list(base.shape)

    def narrow(self, axis, start, size):
        starts, sizes = list(self.starts), list(self.sizes)
        starts[axis] = starts[axis] + start
        sizes[axis] = size
        return View(self.base, starts, sizes)

    def read(self):
        if self.sizes == list(self.base.shape):
            return self.base
        if all(isinstance(start, int) for start in self.starts):
            ends = [start + size for start, size in zip(self.starts, self.sizes)]
            return lax.slice(self.base, self.starts, ends)
        return lax.dynamic_slice(self.base, self.starts, self.sizes)


def total_of(views):
    value = views[0].read().astype(F32)
    for view in views[1:]:
        value = value + view.read().astype(F32)
    return value


def split_on(axis_at):
    return lambda view, bit: view.narrow(axis_at, bit, 1)


def split_rows(axis_at, step, size):
    return lambda view, bit: view.narrow(axis_at, bit * step, size)


def send_half(links, views, axis, mask, choose):
    bit = (lax.axis_index(axis) // mask) % 2
    away = links.hold(1 - bit, (axis, mask))
    send = total_of([choose(view, away) for view in views]).astype(BF16)
    received = links.send(send, axis, xor_pairs(axis, mask), (axis, mask))
    return [choose(view, bit) for view in views], received


def halve(links, views, axis, mask, choose):
    kept, received = send_half(links, views, axis, mask, choose)
    yield [received]
    return kept + [View(received)]


def halve_z(links, views, choose_far, choose_near):
    bit = lax.axis_index("dp") // 4
    away = links.hold(1 - bit, ("dp", 2))
    send = total_of([choose_far(view, away) for view in views]).astype(BF16)
    inward = links.send(send, "dp", INWARD, ("dp", 2))
    yield [inward]
    away = links.hold(1 - bit, "middle")
    send = total_of([choose_far(view, away) for view in views] + [View(inward)]).astype(BF16)
    middle = links.send(send, "dp", MIDDLE, "middle")
    yield [middle]
    views = [choose_far(view, bit) for view in views] + [View(middle)]
    return (yield from halve(links, views, "dp", 2, choose_near))


def reduce_full(links, gradient):
    count, height, breadth = gradient.shape
    rows = height // 8
    slots = Slots(rows)
    by_core = split_rows(4, slots.offset, 2 * slots.size)
    by_y = split_rows(4, slots.size, slots.size)
    by_x = split_on(3)
    views = [View(gradient.reshape(count, 2, 2, 2, rows, breadth))]
    views = yield from halve(links, views, "fsdp", 1, by_core)
    cut = cut_of(breadth)
    first = [view.narrow(5, 0, cut) for view in views]
    second = [view.narrow(5, cut, breadth - cut) for view in views]
    first, got_first = send_half(links, first, "dp", 1, by_x)
    second, got_second = send_half(links, second, "fsdp", 2, by_y)
    yield [got_first, got_second]
    first, second = first + [View(got_first)], second + [View(got_second)]
    first, got_first = send_half(links, first, "fsdp", 2, by_y)
    second, got_second = send_half(links, second, "dp", 1, by_x)
    yield [got_first, got_second]
    first, second = first + [View(got_first)], second + [View(got_second)]
    joined = jnp.concatenate([total_of(first), total_of(second)], axis=-1).astype(BF16)
    views = yield from halve_z(links, [View(joined)], split_on(1), split_on(2))
    return total_of(views).astype(BF16).reshape(count, slots.size, breadth)


def reduce_wide(gradient):
    thin = lax.psum_scatter(gradient.astype(BF16), "fsdp", scatter_dimension=2, tiled=True)
    return lax.psum_scatter(thin.astype(F32), "dp", scatter_dimension=1, tiled=True)


def spread_tokens(rows):
    pair = jnp.concatenate([rows, swap(rows, *YAX)], axis=0)
    return jnp.concatenate([pair, swap(pair, *CORE)], axis=0)


def collect_tokens(partial):
    half = partial.shape[0] // 2
    pair = partial[:half] + swap(partial[half:].astype(BF16), *CORE).astype(F32)
    quarter = half // 2
    return pair[:quarter] + swap(pair[quarter:].astype(BF16), *YAX).astype(F32)


def pick(pair, bit):
    return lax.dynamic_index_in_dim(pair, bit, axis=0, keepdims=False)


def to_latent(pair, y):
    return jnp.concatenate([pick(pair, y), swap(pick(pair, 1 - y), *YAX)], axis=0)


def from_latent(rows, y):
    half = rows.shape[0] // 2
    own = rows[:half]
    other = swap(rows[half:], *YAX)
    return jnp.where(y == 0, jnp.stack([own, other]), jnp.stack([other, own]))


def flatten_all(arrays):
    return jnp.concatenate([matrix.reshape(-1) for matrix in arrays])


def split_all(vector, shapes):
    pieces = []
    offset = 0
    for shape_now in shapes:
        count_now = math.prod(shape_now)
        pieces.append(vector[offset : offset + count_now].reshape(shape_now))
        offset = offset + count_now
    return pieces


def statistics(group, extra, late):
    dp, fsdp = lax.axis_size("dp"), lax.axis_size("fsdp")
    old_sums = jnp.concatenate([jnp.sum(rows, axis=1) for _, _, rows, _ in group])
    master_squares = jnp.concatenate(
        [jnp.sum(after(master, late) ** 2, axis=(1, 2)) for master, _, _, _ in group]
    )
    squares = [gradient * gradient + EPS_SQUARE for _, gradient, _, _ in group]
    row_parts = [jnp.sum(square_block, axis=2) for square_block in squares]
    column_parts = [jnp.sum(square_block, axis=1) for square_block in squares]
    row_sums = split_all(butterfly(flatten_all(row_parts), "fsdp"), [part.shape for part in row_parts])
    over_dp = column_parts + [old_sums / fsdp, master_squares] + ([] if extra is None else [extra])
    over_dp = split_all(butterfly(flatten_all(over_dp), "dp"), [part.shape for part in over_dp])
    column_sums = over_dp[: len(group)]
    totals = [jnp.concatenate([jnp.sum(part, axis=1) for part in column_sums])] + over_dp[len(group) :]
    totals = split_all(butterfly(flatten_all(totals), "fsdp"), [part.shape for part in totals])
    counts = [(part.shape[0],) for part in row_parts]
    square_split, old_split, master_split = [split_all(total, counts) for total in totals[:3]]
    states = []
    for (_, gradient, rows, columns), row_sum, column_sum, square_total, old_total, master_sum in zip(
        group, row_sums, column_sums, square_split, old_split, master_split
    ):
        height, breadth = gradient.shape[1] * dp, gradient.shape[2] * fsdp
        rows_new = DECAY * rows + (1.0 - DECAY) * row_sum / breadth
        columns_new = DECAY * columns + (1.0 - DECAY) * column_sum / height
        mean = (DECAY * old_total + (1.0 - DECAY) * square_total / breadth) / height
        update = gradient * lax.rsqrt(rows_new[:, :, None] * columns_new[:, None, :] / mean[:, None, None])
        states.append((rows_new, columns_new, update, jnp.sum(update * update, axis=(1, 2)), master_sum))
    return states, totals[3] if extra is not None else None


WIDE = 768
MEMBERS = 9


def members_of(arrays):
    return [(at, one, slab.shape[1], slab.shape[2]) for at, slab in enumerate(arrays) for one in range(slab.shape[0])]


def pack_rows(states):
    rows = [jnp.pad(state, ((0, 0), (0, WIDE - state.shape[1]))) for state in states]
    return jnp.pad(jnp.concatenate(rows, axis=0), ((0, 16 - MEMBERS), (0, 0)))


def pack_columns(states):
    rows = [
        jnp.pad(state, ((0, 0), (0, 2 * WIDE - state.shape[1]))).reshape(-1, WIDE) for state in states
    ]
    return jnp.pad(jnp.concatenate(rows, axis=0), ((0, 32 - 2 * MEMBERS), (0, 0)))


def lane_is(index, shape):
    return lax.broadcasted_iota(jnp.int32, shape, 1) == index


def sums_kernel(count, *refs):
    grads, (extra_ref, rows_ref, columns_ref, turn_ref) = refs[:count], refs[count:]
    columns_ref[...] = jnp.zeros(columns_ref.shape, F32)
    turn_ref[...] = jnp.zeros(turn_ref.shape, F32)
    rows_ref[...] = jnp.zeros(rows_ref.shape, F32)
    totals = jnp.zeros((1, WIDE), F32)
    for at, (slab, one, height, breadth) in enumerate(members_of(grads)):
        gradient = grads[slab][one]
        square = gradient * gradient + EPS_SQUARE
        in_row = jnp.sum(square, axis=1, keepdims=True)
        turn_ref[:height, :] += jnp.where(lane_is(at, (height, 128)), in_row, 0.0)
        in_column = jnp.sum(square, axis=0, keepdims=True)
        columns_ref[2 * at : 2 * at + 1, : min(breadth, WIDE)] = in_column[:, :WIDE]
        if breadth > WIDE:
            columns_ref[2 * at + 1 : 2 * at + 2, : breadth - WIDE] = in_column[:, WIDE:]
        totals += jnp.where(lane_is(2 * MEMBERS + at, (1, WIDE)), jnp.sum(in_row), 0.0)
    rows_ref[:16, :] = turn_ref[...].T[:16]
    rows_ref[16:32, :] = extra_ref[...]
    rows_ref[26:27, :] = extra_ref[10:11, :] + totals


def scalar_at(row, index):
    return jnp.sum(jnp.where(lane_is(index, row.shape), row, 0.0))


def updates_of(grads, at, member, turned, columns_ref, mean):
    slab, one, height, breadth = member
    column = columns_ref[2 * at : 2 * at + 1, : min(breadth, WIDE)]
    if breadth > WIDE:
        column = jnp.concatenate([column, columns_ref[2 * at + 1 : 2 * at + 2, : breadth - WIDE]], axis=1)
    row = turned[:height, at : at + 1]
    return grads[slab][one] * lax.rsqrt(row * (column / mean))


def mean_of(scalars, at, height, breadth):
    old, square = scalar_at(scalars, at), scalar_at(scalars, 2 * MEMBERS + at)
    return (DECAY * old + (1.0 - DECAY) * square / breadth) / height


def states_kernel(count, dp, fsdp, *refs):
    grads = refs[:count]
    row_sum_ref, column_sum_ref, old_rows_ref, old_columns_ref = refs[count : count + 4]
    rows_ref, columns_ref, squares_ref, turn_ref = refs[count + 4 :]
    scalars = column_sum_ref[42:43, :]
    rows_ref[...] = jnp.zeros(rows_ref.shape, F32)
    columns_ref[...] = jnp.zeros(columns_ref.shape, F32)
    members = members_of(grads)
    for at, (_, _, height, breadth) in enumerate(members):
        rows_ref[at : at + 1, :] = DECAY * old_rows_ref[at : at + 1, :] + row_sum_ref[at : at + 1, :] * (
            (1.0 - DECAY) / (breadth * fsdp)
        )
        columns_ref[2 * at : 2 * at + 2, :] = DECAY * old_columns_ref[
            2 * at : 2 * at + 2, :
        ] + column_sum_ref[2 * at : 2 * at + 2, :] * ((1.0 - DECAY) / (height * dp))
    turn_ref[:16, :] = rows_ref[...]
    turned = turn_ref[...].T
    found = jnp.zeros((8, 128), F32)
    for at, member in enumerate(members):
        mean = mean_of(scalars, at, member[2] * dp, member[3] * fsdp)
        update = updates_of(grads, at, member, turned, columns_ref, mean)
        found += jnp.where(lane_is(at, (8, 128)), jnp.sum(update * update), 0.0)
    squares_ref[...] = found


def masters_kernel(count, dp, fsdp, *refs):
    grads, masters = refs[:count], refs[count : 2 * count]
    rows_ref, columns_ref, column_sum_ref, squares_ref = refs[2 * count : 2 * count + 4]
    outs, turn_ref = refs[2 * count + 4 : -1], refs[-1]
    scalars = column_sum_ref[42:43, :]
    squares = squares_ref[0:1, :]
    turn_ref[:16, :] = rows_ref[...]
    turned = turn_ref[...].T
    for at, member in enumerate(members_of(grads)):
        slab, one, height, breadth = member
        mean = mean_of(scalars, at, height * dp, breadth * fsdp)
        update = updates_of(grads, at, member, turned, columns_ref, mean)
        entries = height * dp * breadth * fsdp
        row = jnp.zeros((1, 128), F32)
        ratio = jnp.sqrt(row + scalar_at(squares, at) / entries) / CLIP
        scale = jnp.maximum(EPS_SCALE, jnp.sqrt(row + scalar_at(scalars, MEMBERS + at) / entries))
        step = (RATE * scale / jnp.maximum(1.0, ratio))[:, :1]
        outs[slab][one] = masters[slab][one] - step * update


def vmem_call(kernel, operands, shapes, scratch):
    return pl.pallas_call(
        kernel,
        out_shape=[jax.ShapeDtypeStruct(shape, F32) for shape in shapes],
        in_specs=[pl.BlockSpec(memory_space=pltpu.VMEM)] * len(operands),
        out_specs=[pl.BlockSpec(memory_space=pltpu.VMEM)] * len(shapes),
        scratch_shapes=[pltpu.VMEM(shape, F32) for shape in scratch],
        compiler_params=pltpu.CompilerParams(vmem_limit_bytes=40 << 20),
        cost_estimate=pl.CostEstimate(flops=20000000, bytes_accessed=10000000, transcendentals=1200000),
    )(*operands)


def both_axes(value):
    return butterfly(butterfly(value, "fsdp"), "dp")


def fused_update(group, gains_part, late):
    dp, fsdp = lax.axis_size("dp"), lax.axis_size("fsdp")
    masters = [master for master, _, _, _ in group]
    grads = [gradient for _, gradient, _, _ in group]
    rows, columns = [member[2] for member in group], [member[3] for member in group]
    old_sums = jnp.concatenate([jnp.sum(state, axis=1) for state in rows]) / fsdp
    master_squares = jnp.concatenate([jnp.sum(after(master, late) ** 2, axis=(1, 2)) for master in masters])
    scalars = jnp.pad(jnp.concatenate([old_sums, master_squares])[None], ((0, 5), (0, WIDE - 2 * MEMBERS)))
    gains_rows = jnp.pad(gains_part.reshape(10, -1), ((0, 0), (0, WIDE - D // 2)))
    extra = jnp.concatenate([gains_rows, scalars], axis=0)
    old_rows, old_columns = pack_rows(rows), pack_columns(columns)
    count = len(group)
    packed_rows, packed_columns = vmem_call(
        functools.partial(sums_kernel, count), [*grads, extra], [(32, WIDE), (32, WIDE)], [(WIDE, 128)]
    )
    row_sums = butterfly(packed_rows, "fsdp")
    column_sums = butterfly(jnp.concatenate([packed_columns, row_sums[16:]], axis=0), "dp")
    new_rows, new_columns, squares = vmem_call(
        functools.partial(states_kernel, count, dp, fsdp),
        [*grads, row_sums, column_sums, old_rows, old_columns],
        [(16, WIDE), (32, WIDE), (8, 128)],
        [(128, WIDE)],
    )
    squares = both_axes(squares)
    new_masters = vmem_call(
        functools.partial(masters_kernel, count, dp, fsdp),
        [*grads, *masters, new_rows, new_columns, column_sums, squares],
        [master.shape for master in masters],
        [(128, WIDE)],
    )
    finished = []
    at = 0
    for which, (master, gradient, _, _) in enumerate(group):
        many, height, breadth = master.shape
        row_out = new_rows[at : at + many, :height]
        column_out = new_columns[2 * at : 2 * (at + many)].reshape(many, -1)[:, :breadth]
        finished.append([new_masters[which], row_out, column_out, gradient])
        at += many
    gain_total = column_sums[32:42, : D // 2].reshape(5, D)
    return finished, gain_total


def shards(
    latents,
    skip_input,
    text_tokens,
    cotangent,
    timesteps,
    text_lengths,
    positions,
    skip_weight,
    skip_rows,
    skip_columns,
    square_weight,
    square_rows,
    square_columns,
    self_weight,
    self_rows,
    self_columns,
    output_weight,
    output_rows,
    output_columns,
    text_weight,
    text_rows,
    text_columns,
    up_weight,
    up_rows,
    up_columns,
    down_weight,
    down_rows,
    down_columns,
    norm_gains,
    gain_state,
):
    dp = lax.axis_size("dp")
    d_at = lax.axis_index("dp")
    f_at = lax.axis_index("fsdp")
    y_at = f_at // 2
    c_at = f_at % 2
    index = jnp.stack([d_at, f_at]).astype(jnp.int32)

    dp_masks = masks_of("dp")

    fsdp = lax.axis_size("fsdp")
    every = ("dp", "fsdp")
    rows_d = up_weight.shape[0]
    chunk = down_weight.shape[0] // 4
    per_f = up_weight.shape[1] // (4 * chunk)
    quick = fits(rows_d)
    links = Links()
    skip_slots, wide_slots = Slots(skip_weight.shape[0]), Slots(rows_d)
    down_slots = Slots(down_weight.shape[0], True)
    text_slots = Slots(text_weight.shape[0], True)
    skip_block = skip_weight.astype(BF16)[None]
    self_block = self_weight.astype(BF16)[None]
    cross_block = jnp.stack([output_weight[0], square_weight[1], output_weight[1]]).astype(BF16)

    def advance(*flows):
        for flow in flows:
            flow.step()

    text_local = to_latent(text_tokens, y_at)
    places = to_latent(jnp.swapaxes(positions, 1, 2), y_at).T
    text_count = pick(text_lengths, y_at)
    steps = double(timesteps[None], [("dp", mask) for mask in dp_masks])
    rows_q = square_weight.shape[1]
    columns_q = square_weight.shape[2]

    if quick:
        skip_slot = slot_rows(exchange([slot_pieces(skip_block, skip_slots)])[0], skip_slots, 1)
        skip_slot = after(skip_slot, steps, places, text_local)
        skip_flow = Flow(gather_full(links, index, skip_slot, [(0, 1, skip_slots)]))
        skip_flow.step()
        early = skip_flow.pending[0]
    else:
        early = None
    joined = jnp.concatenate([to_latent(latents, y_at), to_latent(skip_input, y_at)], axis=-1).astype(F32)
    shift_block = square_weight[0].astype(BF16)[None]
    if quick:
        self_part, shift_part = after((self_block, shift_block), early)
        got = exchange([slot_pieces(self_part, wide_slots), slot_pieces(shift_part, wide_slots)])
        self_slot = jnp.concatenate([slot_rows(part, wide_slots, 1) for part in got], axis=-1)
        self_flow = Flow(gather_halves(links, index, self_slot, wide_slots))
        advance(skip_flow)
        advance(skip_flow, self_flow)
        advance(skip_flow, self_flow)
        early = skip_flow.pending[0]
    text_part, down_part, up_part, cross_part = after(
        (
            text_weight.astype(BF16)[None],
            down_weight.astype(BF16)[None],
            up_weight.astype(BF16),
            cross_block,
        ),
        early,
    )
    columns_h = per_f * chunk
    up_cuts = [
        [up_part[:, (4 * block + f) * chunk : (4 * block + f + 1) * chunk] for block in range(per_f)]
        for f in range(4)
    ]
    pieces = [
        slot_pieces(down_part, down_slots),
        jnp.stack([jnp.concatenate(cuts, axis=1) for cuts in up_cuts]),
        slot_pieces(text_part, text_slots),
    ]
    if quick:
        pieces.append(slot_pieces(cross_part, wide_slots))
    got = exchange(pieces)
    down_slot = slot_rows(got[0], down_slots, 1)[0]
    up_block = jnp.concatenate([got[1][f] for f in range(4)], axis=1)
    text_slot = slot_rows(got[2], text_slots, 1)
    if quick:
        text_flow = Flow(gather_full(links, index, text_slot, [(0, 1, text_slots)]))
        cross_flow = Flow(gather_halves(links, index, slot_rows(got[3], wide_slots, 3), wide_slots))
        up_flow = Flow(gather_dp(links, index, up_block, True))
        down_flow = Flow(gather_dp(links, index, down_slot, False))
        advance(skip_flow, self_flow)
        advance(self_flow)
    else:
        text_full = lax.all_gather(text_slot[0], every, axis=0, tiled=True)
        down_full = lax.all_gather(down_slot, "dp", axis=0, tiled=True)
    embed_own = jax.nn.silu(time_embed(pick(timesteps, y_at)[None], D)).astype(BF16)

    if quick:
        skip_full = skip_flow.finish()[0][0]
    else:
        skip_full = gather_wide(skip_block)[0]

    normed_skip, pull_skip = jax.vjp(skip_norm, joined, norm_gains[0:2].reshape(-1))
    lowered_skip = normed_skip.astype(BF16)
    stream = matmul(lowered_skip, skip_full)
    links.gate = stream
    if quick:
        advance(self_flow)
        links.gate = None
        advance(cross_flow)
        links.gate = stream
        advance(text_flow)
        advance(text_flow, up_flow)
        both_full = self_flow.finish()[0]
        self_full, shift_full = both_full[:, : 3 * D], both_full[:, 3 * D :]
    else:
        self_full, shift_full = gather_wide(self_block)[0], gather_wide(shift_block)[0]
    shift_row = matmul(embed_own, shift_full)
    normed_self, pull_self_norm = jax.vjp(modulated, stream, norm_gains[2], shift_row)
    lowered_self = normed_self.astype(BF16)
    if quick:
        links.gate = None
        lowered_self = cross_flow.step(lowered_self)
    joint = matmul(lowered_self, self_full)
    links.gate = joint
    if quick:
        advance(cross_flow)
        links.gate = joint
        advance(text_flow, up_flow)
        advance(text_flow, cross_flow, up_flow, down_flow)
        advance(text_flow, down_flow)

    def prepare(linear):
        return head_prep(linear, places)

    query_rows, pull_query = jax.vjp(prepare, joint[:, :D])
    key_local, pull_key = jax.vjp(prepare, joint[:, D : 2 * D])
    queries = query_rows.astype(BF16)
    key_value = jnp.stack([key_local.astype(BF16), joint[:, 2 * D :].astype(BF16)])
    key_value = jnp.concatenate([key_value, swap(key_value, *CORE)], axis=1)
    key_all, value_all = key_value[0], key_value[1]

    upstream = to_latent(after(cotangent, stream), y_at)
    upstream_pair = jnp.concatenate([upstream, swap(upstream, *YAX)], axis=0)
    upstream_far = swap(upstream_pair, *CORE)
    upstream_all = jnp.concatenate([upstream_pair, upstream_far], axis=0)
    attended, self_logsum = attend_forward(queries, key_all, value_all, None)
    attended = after(attended, upstream_far)
    links.gate = attended
    if quick:
        text_full = text_flow.finish()[0][0]
        advance(up_flow, cross_flow, down_flow)
        cross_full = cross_flow.finish()
    else:
        cross_full = gather_wide(cross_block)
    text_joint = matmul(text_local, text_full)
    text_key_local, pull_text_key = jax.vjp(head_norm, text_joint[:, :D])
    text_kv = jnp.stack([text_key_local.astype(BF16), text_joint[:, D:].astype(BF16)])
    text_kv = jnp.concatenate([text_kv, swap(text_kv, *CORE)], axis=1)
    text_key_all, text_value_all = text_kv[0], text_kv[1]

    out_self, square_cross, out_cross = cross_full[0], cross_full[1], cross_full[2]
    self_stream = stream + matmul(attended, out_self)
    normed_cross, pull_cross_norm = jax.vjp(gained, self_stream, norm_gains[3])
    lowered_cross = normed_cross.astype(BF16)
    cross_linear = matmul(lowered_cross, square_cross)
    cross_query_rows, pull_cross_query = jax.vjp(prepare, cross_linear)
    cross_queries = cross_query_rows.astype(BF16)
    own_text = text_tokens.shape[1]
    text_places = jnp.concatenate(
        [(f_at ^ mask) * own_text + jnp.arange(own_text) for mask in (0, 2, 1, 3)]
    )
    valid_keys = text_places < text_count
    cross_attended, cross_logsum = attend_forward(cross_queries, text_key_all, text_value_all, valid_keys)
    cross_stream = self_stream + matmul(cross_attended, out_cross)
    normed_mlp, pull_mlp_norm = jax.vjp(gained, cross_stream, norm_gains[4])
    lowered_mlp = spread_tokens(normed_mlp.astype(BF16))
    if quick:
        up_full = up_flow.finish().reshape(dp * rows_d, -1)
        down_full = down_flow.finish().reshape(dp * chunk, D)
    else:
        up_full = lax.all_gather(up_block, "dp", axis=0, tiled=True)
    hidden_pre = matmul(lowered_mlp, up_full)
    hidden_rows, pull_gelu = jax.vjp(gelu_tanh, hidden_pre)
    hidden_low = hidden_rows.astype(BF16)
    block_partial = matmul(hidden_low, down_full)

    back = Links()

    grad_hidden = matmul_right(upstream_all, down_full)
    grad_pre = pull_gelu(grad_hidden)[0].astype(BF16)
    mlp_partial = matmul_right(grad_pre, up_full)
    term_down = matmul_left(hidden_low, upstream_all).astype(BF16)
    down_rows_sum = lax.psum_scatter(term_down, "dp", scatter_dimension=0, tiled=True)
    term_up = matmul_left(lowered_mlp, grad_pre).astype(BF16)
    up_rows_sum = lax.psum_scatter(term_up, "dp", scatter_dimension=0, tiled=True)
    grad_mlp_in = after(collect_tokens(mlp_partial), term_down, term_up)
    block_rows = (cross_stream + collect_tokens(after(block_partial, grad_mlp_in))).astype(BF16)
    block_output = from_latent(block_rows, y_at)

    grad_cross_part, grad_gain_mlp = pull_mlp_norm(grad_mlp_in)
    grad_cross_stream = upstream.astype(F32) + grad_cross_part
    cross_low = grad_cross_stream.astype(BF16)
    grad_cross_att = matmul_right(cross_low, out_cross).astype(BF16)
    grad_cross_q, grad_text_key, grad_text_value = attend_backward(
        cross_queries, text_key_all, text_value_all, valid_keys, cross_logsum, grad_cross_att
    )
    grad_text_kv = jnp.stack([grad_text_key, grad_text_value])
    text_half = grad_text_kv.shape[1] // 2
    grad_text_got = swap(grad_text_kv[:, text_half:].astype(BF16), *CORE)
    grad_cross_linear = pull_cross_query(grad_cross_q)[0].astype(BF16)
    grad_cross_in = matmul_right(grad_cross_linear, square_cross)
    grad_self_part, grad_gain_cross = pull_cross_norm(grad_cross_in)
    grad_self_stream = grad_cross_stream + grad_self_part
    self_low = grad_self_stream.astype(BF16)
    grad_self_att = matmul_right(self_low, out_self).astype(BF16)
    cross_terms = lax.dot_general(
        jnp.stack([attended, lowered_cross, cross_attended]),
        jnp.stack([self_low, grad_cross_linear, cross_low]),
        (((1,), (1,)), ((0,), (0,))),
        preferred_element_type=F32,
    ).astype(BF16)
    if quick:
        cross_back = Flow(reduce_full(back, cross_terms))
        cross_back.step()
    grad_query, grad_key_all, grad_value_all = attend_backward(
        queries, key_all, value_all, None, self_logsum, grad_self_att
    )
    grad_kv = jnp.stack([grad_key_all, grad_value_all])
    token_half = grad_kv.shape[1] // 2
    grad_kv_got = swap(grad_kv[:, token_half:].astype(BF16), *CORE)

    grad_text_local = grad_text_kv[:, :text_half] + grad_text_got.astype(F32)
    text_grad_joint = jnp.concatenate(
        [pull_text_key(grad_text_local[0])[0], grad_text_local[1]], axis=-1
    ).astype(BF16)
    term_text = matmul_left(text_local, text_grad_joint).astype(BF16)
    text_rows_sum = lax.psum_scatter(after(term_text, up_rows_sum), every, scatter_dimension=0, tiled=True)

    if quick:
        grad_kv_got = cross_back.step(grad_kv_got)
    grad_kv_local = grad_kv[:, :token_half] + grad_kv_got.astype(F32)
    grad_joint = jnp.concatenate(
        [pull_query(grad_query)[0], pull_key(grad_kv_local[0])[0], grad_kv_local[1]], axis=-1
    ).astype(BF16)
    term_self = matmul_left(lowered_self, grad_joint).astype(BF16)[None]
    if quick:
        self_back = Flow(reduce_full(back, term_self))
        self_back.step()
    grad_self_in = matmul_right(grad_joint, self_full)
    grad_stream_part, grad_gain_self, grad_shift = pull_self_norm(grad_self_in)
    grad_stream = grad_self_stream + grad_stream_part
    stream_low = grad_stream.astype(BF16)
    if quick:
        stream_low = self_back.step(cross_back.step(stream_low))
    term_skip = matmul_left(lowered_skip, stream_low).astype(BF16)[None]
    if quick:
        skip_back = Flow(reduce_full(back, term_skip))
        skip_back.step()
    grad_skip_in = matmul_right(stream_low, skip_full)
    if quick:
        advance(cross_back, self_back, skip_back, cross_back, skip_back)
    grad_joined, grad_gain_skip = pull_skip(grad_skip_in)
    first_pieces = [
        back_pieces(text_rows_sum.astype(BF16)[None]),
        back_pieces(down_rows_sum.astype(BF16)[None]),
        jnp.swapaxes(up_rows_sum.astype(BF16).reshape(rows_d, 4, per_f * chunk), 0, 1),
    ]
    if quick:
        first_pieces.append(back_pieces(cross_back.finish()))
    latents_grad = from_latent(grad_joined[:, :D].astype(BF16), y_at)
    skip_input_grad = from_latent(grad_joined[:, D:].astype(BF16), y_at)

    quiet = None
    if quick:
        advance(self_back, skip_back, self_back, skip_back)
        quiet = skip_back.pending[0]
        last_pieces = [back_pieces(self_back.finish()), back_pieces(skip_back.finish())]
        first_pieces += last_pieces
    got = exchange(first_pieces, quiet)
    text_sum = back_block(got[0], text_slots, 1).astype(F32)
    down_sum = back_block(got[1], down_slots, 1).astype(F32)
    up_cuts = [
        got[2][f][:, block * chunk : (block + 1) * chunk] for block in range(per_f) for f in range(4)
    ]
    up_sum = jnp.concatenate(up_cuts, axis=1).astype(F32)[None]
    if quick:
        cross_sum = back_block(got[3], wide_slots, 3).astype(F32)
    else:
        cross_sum = reduce_wide(cross_terms)

    embed_all = jax.nn.silu(time_embed(steps.reshape(-1), D)).astype(BF16)
    embed_part = lax.dynamic_slice_in_dim(embed_all, d_at * rows_q, rows_q, axis=1)
    grad_shift = after(grad_shift.reshape(1, D), quiet)
    grad_shift = grad_shift + swap(grad_shift, *CORE)
    other_shift = swap(grad_shift, *YAX)
    shift_pair = jnp.where(
        y_at == 0,
        jnp.concatenate([grad_shift, other_shift]),
        jnp.concatenate([other_shift, grad_shift]),
    )
    shift_pair = lax.dynamic_slice_in_dim(shift_pair, f_at * columns_q, columns_q, axis=1)
    shift_grads = double(shift_pair[None], [("dp", mask) for mask in dp_masks]).reshape(-1, columns_q)
    modulate_sum = lax.dot_general(
        embed_part.astype(F32),
        shift_grads,
        (((0,), (0,)), ((), ())),
        precision=lax.Precision.HIGHEST,
        preferred_element_type=F32,
    )

    gains_part = jnp.concatenate(
        [grad_gain_skip.reshape(2, -1), grad_gain_self[None], grad_gain_cross[None], grad_gain_mlp[None]],
        axis=0,
    )
    square_sum = jnp.stack([modulate_sum, cross_sum[1]])
    output_sum = jnp.stack([cross_sum[0], cross_sum[2]])
    early_group = [
        (square_weight, square_sum, square_rows, square_columns),
        (output_weight, output_sum, output_rows, output_columns),
        (text_weight[None], text_sum, text_rows[None], text_columns[None]),
        (up_weight[None], up_sum, up_rows[None], up_columns[None]),
        (down_weight[None], down_sum, down_rows[None], down_columns[None]),
    ]
    if quick:
        self_sum = back_block(got[4], wide_slots, 1).astype(F32)
        skip_sum = back_block(got[5], skip_slots, 1).astype(F32)
    else:
        self_sum, skip_sum = reduce_wide(term_self), reduce_wide(term_skip)
    late_group = [
        (skip_weight[None], skip_sum, skip_rows[None], skip_columns[None]),
        (self_weight[None], self_sum, self_rows[None], self_columns[None]),
    ]
    groups = late_group + early_group
    if quick:
        finished, gain_total = fused_update(groups, gains_part, joint)
    else:
        states, gain_total = statistics(groups, gains_part, joint)
        update_squares = jnp.concatenate([state[3] for state in states])
        update_all = butterfly(butterfly(update_squares, "fsdp"), "dp")
        update_split = split_all(update_all, [state[3].shape for state in states])
        finished = []
        for (master, gradient, _, _), state, update_sum in zip(groups, states, update_split):
            rows_new, columns_new, update, _, master_sum = state
            entries = gradient.shape[1] * dp * gradient.shape[2] * fsdp
            ratio = jnp.sqrt(update_sum / entries) / CLIP
            step_scale = jnp.maximum(EPS_SCALE, jnp.sqrt(master_sum / entries))
            master_new = master - (RATE * step_scale / jnp.maximum(1.0, ratio))[:, None, None] * update
            finished.append([master_new, rows_new, columns_new, gradient])
    skip_done, self_done, square_done, output_done, text_done, up_done, down_done = finished
    gain_state_new = DECAY * gain_state + (1.0 - DECAY) * (gain_total * gain_total + EPS_SQUARE)
    gain_update = gain_total * lax.rsqrt(gain_state_new)
    gain_ratio = jnp.sqrt(jnp.mean(gain_update * gain_update)) / CLIP
    gain_scale = jnp.maximum(EPS_SCALE, jnp.sqrt(jnp.mean(norm_gains * norm_gains)))
    gains_new = norm_gains - RATE * gain_scale * gain_update / jnp.maximum(1.0, gain_ratio)
    results = [block_output, latents_grad, skip_input_grad]
    for which, group in enumerate(
        [skip_done, square_done, self_done, output_done, text_done, up_done, down_done]
    ):
        if which in (1, 3):
            results.extend(group)
        else:
            results.extend(item[0] for item in group)
    return tuple(results) + (gains_new, gain_state_new, gain_total)


def solution(mesh):
    matrix, row, column = P("dp", "fsdp"), P("dp"), P("fsdp")
    pair, pair_row, pair_column = P(None, "dp", "fsdp"), P(None, "dp"), P(None, "fsdp")
    tokens = P("dp", "fsdp", None)
    kinds = (False, True, False, True, False, False, False)
    in_specs = [tokens] * 4 + [P("dp"), P("dp"), P("dp", None, "fsdp")]
    out_specs = [tokens] * 3
    for paired in kinds:
        if paired:
            in_specs += [pair, pair_row, pair_column]
            out_specs += [pair, pair_row, pair_column, pair]
        else:
            in_specs += [matrix, row, column]
            out_specs += [matrix, row, column, matrix]
    return jax.shard_map(
        shards,
        mesh=mesh,
        in_specs=tuple(in_specs + [P(), P()]),
        out_specs=tuple(out_specs + [P(), P(), P()]),
        check_vma=False,
    )
```
